128 devices in a mesh: pair: 16 (over x_hi, y, core), aux: 8 (over x_lo, z).
Axes of the slice: x: 4 (x_hi: 2, x_lo: 2; x = x_hi * 2 + x_lo), y: 4, z: 4, core: 2. Of those that a mesh axis runs over, the one named last changes fastest.
Arguments:
- slab: bfloat16 [180224, 8192], P('pair', 'aux')
- density: bfloat16 [512, 64, 128], P(('pair', 'aux')), may hold values from -6 to 6
- block_list: int32 [1408], P('pair'), may hold values from 0 to 511
- block_sizes: int32 [1408], P('pair'), may hold values from 32 to 128, as said below
- metric: float32 [8192, 384], P('aux'), as said below
Outputs:
- coulomb: bfloat16 [1408, 64, 128], P(('pair', 'aux'))
- coeffs: float32 [64, 8192], P(None, 'aux')
The draws below stay inside these ranges and needn't reach their ends.
Inputs may be any that keep to these rules, and one draw needn't show every extreme that they name: `block_sizes`: in each pair group's 88 slots at least one slot has 128 live pair functions. `metric`: each row's entry at column 128 + (row mod 128) exceeds the sum of the magnitudes of the row's other entries.
All inputs are finite; a program needn't handle non-finite values.
Results may differ from the reference program's by a relative error of at most 0.0042.
Values may be sent and summed in bfloat16 or wider, within the bound.
A program may use at most 128 MiB of HBM per device.

```python
import math
import jax
import jax.numpy as jnp
import numpy as np
from jax import lax

NDENS = 64
BS = 128
HB = 128
ITERS = 4
NBLK = 88
NAUX = 8192
SLOTS = 1408
NDB = 512


def draw_slab(key, part):
    key = jax.random.fold_in(key, 31)
    first_key, second_key, third_key = jax.random.split(key, 3)
    row_total = SLOTS * BS
    spread = 4.0 * row_total ** (-0.5)
    common = 0.63 * row_total ** (-0.5)
    independent = jax.random.truncated_normal(first_key, -6.0, 6.0, (row_total, NAUX), jnp.float32) * spread
    row_part = jax.random.truncated_normal(second_key, -6.0, 6.0, (row_total, 1), jnp.float32) * common
    phase = jax.random.uniform(third_key, (), jnp.float32, 0.0, 2.0 * math.pi)
    columns = jnp.arange(NAUX, dtype=jnp.float32)
    wave = jnp.cos(columns * (math.pi / (4 * HB)) + phase)
    return (independent + row_part * wave[None, :]).astype(jnp.bfloat16)


def draw_block_sizes(key, part):
    key = jax.random.fold_in(key, 11)
    first_key, second_key = jax.random.split(key)
    groups = SLOTS // NBLK
    base = jax.random.randint(first_key, (groups, NBLK), BS // 4, BS + 1)
    position = jax.random.randint(second_key, (groups, 1), 0, NBLK)
    full_slot = jnp.arange(NBLK, dtype=jnp.int32)[None, :] == position
    return jnp.where(full_slot, BS, base).reshape(groups * NBLK).astype(jnp.int32)


def draw_metric(key, part):
    key = jax.random.fold_in(key, 23)
    first_key, second_key = jax.random.split(key)
    lowest = 0.6
    highest = 1.2
    off_band = jax.random.uniform(first_key, (NAUX, 3 * HB), jnp.float32, lowest, 1.0) * (0.95 / (3 * HB - 1))
    diag_vals = jax.random.uniform(second_key, (NAUX, 1), jnp.float32, 1.0, highest)
    columns = jnp.arange(3 * HB, dtype=jnp.int32)[None, :]
    row_index = jnp.arange(NAUX, dtype=jnp.int32)[:, None]
    return jnp.where(columns == HB + row_index % HB, diag_vals, off_band).astype(jnp.float32)


def set_ends(drawn, key, least, high):
    spot = [jax.random.randint(jax.random.fold_in(key, axis), (), 0, length) for axis, length in enumerate(drawn.shape)]
    widest = drawn.shape.index(max(drawn.shape))
    next_to = spot[:widest] + [(spot[widest] + 1) % drawn.shape[widest]] + spot[widest + 1:]
    return drawn.at[tuple(spot)].set(least).at[tuple(next_to)].set(high)


def shard_levels(own_key, dims, cuts, smallest, largest):
    level = 1.0
    for dim, parts in cuts:
        heights = jax.random.uniform(jax.random.fold_in(jax.random.fold_in(own_key, 6), dim), (parts,), jnp.float32, smallest / len(cuts), largest / len(cuts))
        level = level * jnp.repeat(jnp.exp(heights), dims[dim] // parts).reshape((-1,) + (1,) * (len(dims) - 1 - dim))
    return level


def cumulative_ranks(amount, slope):
    weights = [(1 << 20) // math.isqrt(standing ** slope) + 1 for standing in range(1, amount + 1)]
    scale = 1 + sum(weights) // (1 << 30)
    return np.cumsum(np.array([max(1, weight // scale) for weight in weights]))


def ranked_ids(key, extent, amount, skew):
    table = cumulative_ranks(amount, skew)
    lot = jax.random.randint(jax.random.fold_in(key, 1), extent, 0, int(table[amount - 1]))
    rank = jnp.searchsorted(jnp.asarray(table, jnp.int32), lot, side="right")
    return jax.random.permutation(jax.random.fold_in(key, 2), amount)[rank].astype(jnp.int32)


def normal_values(rng, shape, width, most, cuts=(), held_as=jnp.bfloat16):
    drawn = jax.random.normal(rng, shape, jnp.float32) * width
    if len(cuts) > 0:
        drawn = shard_levels(rng, shape, cuts, -0.22, 0.18) * drawn
    return jnp.clip(drawn, min=-most, max=most).astype(held_as)


def setup_inputs(seed: int = 0) -> dict:
    arg_keys = jax.random.split(jax.random.key(seed), 6)
    slab = draw_slab(jax.random.fold_in(arg_keys[5], 71), 0)
    density = normal_values(arg_keys[1], (NDB, NDENS, BS), 1.0, 6.0, ((0, 128),))
    block_list = set_ends(ranked_ids(arg_keys[2], (SLOTS,), NDB, 2), jax.random.fold_in(arg_keys[2], 3), 0, NDB - 1).astype(jnp.int32)
    block_sizes = draw_block_sizes(jax.random.fold_in(arg_keys[5], 71), 0)
    metric = draw_metric(jax.random.fold_in(arg_keys[5], 71), 0)
    return dict(slab=slab, density=density, block_list=block_list, block_sizes=block_sizes, metric=metric)


def band_apply(metric, values_in):
    count_aux = values_in.shape[1]
    padded = jnp.pad(values_in, ((0, 0), (HB, HB)))
    windows = jnp.stack([padded[:, block_index * HB:block_index * HB + 3 * HB] for block_index in range(count_aux // HB)])
    blocks = metric.reshape(count_aux // HB, HB, 3 * HB)
    result = jnp.einsum("bpc,bdc->dbp", blocks, windows, precision=lax.Precision.HIGHEST)
    return result.reshape(values_in.shape[0], count_aux)


def jacobi_solve(fit_total, metric):
    row_index = jnp.arange(metric.shape[0], dtype=jnp.int32)
    diagonal = jnp.take_along_axis(metric, (HB + row_index % HB)[:, None], axis=1)[:, 0]
    coeffs = fit_total / diagonal
    for sweep in range(ITERS):
        coeffs = coeffs + (fit_total - band_apply(metric, coeffs)) / diagonal
    return coeffs


def reference(slab, density, block_list, block_sizes, metric):
    live_rows = jnp.arange(BS, dtype=jnp.int32)[None, :] < block_sizes[:, None]
    picked = jnp.where(live_rows[:, None, :], density[block_list], jnp.zeros((), jnp.bfloat16)).astype(jnp.bfloat16)
    group_count = SLOTS // NBLK

    def add_group(group, running):
        rows_here = lax.dynamic_slice_in_dim(slab, group * NBLK * BS, NBLK * BS, 0)
        dens_here = lax.dynamic_slice_in_dim(picked, group * NBLK, NBLK, 0)
        dens_flat = dens_here.transpose(1, 0, 2).reshape(NDENS, NBLK * BS)
        return running + jnp.dot(dens_flat, rows_here, preferred_element_type=jnp.float32)

    fit_total = lax.fori_loop(0, group_count, add_group, jnp.zeros((NDENS, NAUX), jnp.float32))
    coeffs = jacobi_solve(fit_total, metric)
    coeff_b = coeffs.astype(jnp.bfloat16)

    def group_coulomb(group):
        rows_here = lax.dynamic_slice_in_dim(slab, group * NBLK * BS, NBLK * BS, 0)
        product = jnp.dot(coeff_b, rows_here.T, preferred_element_type=jnp.float32)
        return product.reshape(NDENS, NBLK, BS).transpose(1, 0, 2)

    stacked = lax.map(group_coulomb, jnp.arange(group_count, dtype=jnp.int32))
    coulomb = stacked.reshape(SLOTS, NDENS, BS)
    coulomb = jnp.where(live_rows[:, None, :], coulomb, jnp.zeros((), jnp.float32)).astype(jnp.bfloat16)
    return coulomb, coeffs
```

```python
import jax
import jax.numpy as jnp
from jax import lax
from jax.experimental import pallas as pl
from jax.experimental.pallas import tpu as pltpu
from jax.sharding import PartitionSpec as P

F32 = jnp.float32
BF16 = jnp.bfloat16
BS = 128
HB = 128
ND = 64
SLOTS = 88
OWN = 11
AUX = 1024
HALF = 512
ROWS = SLOTS * BS
CHUNK = 1024
NCHUNK = ROWS // CHUNK

PARTS = (
    (0, 6, 0, (0, 1, 2)),
    (6, 5, 768, (1, 2, 0)),
    (11, 5, 1408, (2, 0, 1)),
)


def mod(value, size):
    return lax.rem(value + size, size)


def kernel(block_list, block_sizes, density, slab, metric, coulomb, coeffs, *scratch):
    (slab_v, held, picked, acc, sib_acc, fit_send, fit_recv, mw, wh, wl, u0, u, lh,
     own_u, halo, call, cb, opp_send, opp_recv, nb_send, nb_recv, x_send, x_recv, mine,
     index, slab_sem, local_sem, send_sem, recv_sem) = scratch

    pair = lax.axis_index("pair")
    aux = lax.axis_index("aux")
    core = lax.rem(pair, 2)
    chip = pair // 2
    x = (chip // 4) * 2 + aux // 4
    y = lax.rem(chip, 4)
    z = lax.rem(aux, 4)

    def device(coords, at_core):
        ax, ay, az = coords
        return (((ax // 2) * 4 + ay) * 2 + at_core, lax.rem(ax, 2) * 4 + az)

    def moved(dim, by):
        coords = [x, y, z]
        coords[dim] = mod(coords[dim] + by, 4)
        return device(coords, core)

    sibling = device([x, y, z], 1 - core)
    ext_aux = mod(aux + 2 * core - 1, 8)
    ext = (chip * 2 + (1 - core), ext_aux)
    chips = [(mod(chip + o, 8) * 2 + core, aux) for o in range(1, 8)]
    x_mate = (pair, mod(aux + 4, 8))

    slab_copies = []
    for n in range(NCHUNK):
        rows = pl.ds(n * CHUNK, CHUNK)
        slab_copies.append(pltpu.make_async_copy(slab.at[rows, :], slab_v.at[rows, :], slab_sem.at[n]))

    own_metric = pltpu.make_async_copy(
        metric.at[pl.ds(pl.multiple_of(core * 128, 128), 896), :],
        mw.at[pl.ds(pl.multiple_of(384 - core * 384, 128), 896), :],
        local_sem.at[0],
    )
    own_metric.start()

    def place(part, i3, i2, i1, at_core):
        _, tiles, base, _ = PARTS[part]
        return base + (((at_core * 4 + i3) * 4 + i2) * 4 + i1) * tiles

    def spot(part):
        order = PARTS[part][3]
        coords = (x, y, z)
        return coords[order[0]], coords[order[1]], coords[order[2]]

    own_tiles = []
    for part, (first, tiles, _, _) in enumerate(PARTS):
        i1, i2, i3 = spot(part)
        copy = pltpu.make_async_copy(
            density.at[pl.ds(first, tiles)],
            held.at[pl.ds(place(part, i3, i2, i1, core), tiles)],
            local_sem.at[1 + part],
        )
        copy.start()
        own_tiles.append(copy)
    for copy in slab_copies:
        copy.start()

    barrier = pltpu.get_barrier_semaphore()
    partners = [moved(d, s) for d in range(3) for s in (1, -1)] + [sibling, ext, x_mate] + chips
    for partner in partners:
        pl.semaphore_signal(barrier, inc=1, device_id=partner, device_id_type=pl.DeviceIdType.MESH)
    pl.semaphore_wait(barrier, len(partners))

    count = [0]
    sent = []

    def send(src, dst, to):
        n = count[0]
        count[0] += 1
        copy = pltpu.make_async_remote_copy(
            src_ref=src, dst_ref=dst, send_sem=send_sem.at[n], recv_sem=recv_sem.at[n],
            device_id=to, device_id_type=pl.DeviceIdType.MESH,
        )
        copy.start()
        sent.append(copy)
        return n

    def arrived(n, ref):
        pltpu.make_async_remote_copy(
            src_ref=ref, dst_ref=ref, send_sem=send_sem.at[n], recv_sem=recv_sem.at[n],
            device_id=sibling, device_id_type=pl.DeviceIdType.MESH,
        ).wait_recv()

    def window(start, size):
        return held.at[pl.ds(start, size)]

    sib_waits = []

    def to_sibling(part, start, size):
        _, tiles, _, _ = PARTS[part]
        ref = window(start, size)
        n = send(ref, ref, sibling)
        other = start + (1 - 2 * core) * 64 * tiles
        sib_waits.append((n, window(other, size)))

    class Ring:
        def __init__(self, part, level, start_of, size, cut):
            self.part, self.start_of, self.size, self.cut = part, start_of, size, cut
            self.dim = PARTS[part][3][level]
            self.at = (x, y, z)[self.dim]

        def piece(self, by):
            return self.start_of(mod(self.at + by, 4))

        def start(self, src=None):
            ref = window(self.piece(0), self.size)
            src = ref if src is None else src
            self.up = send(src, ref, moved(self.dim, 1))
            self.down = send(src, ref, moved(self.dim, -1))

        def middle(self):
            arrived(self.up, window(self.piece(-1), self.size))
            low = window(self.piece(-1), self.cut)
            self.up_far = send(low, low, moved(self.dim, 1))
            arrived(self.down, window(self.piece(1), self.size))
            high = window(self.piece(1) + self.cut, self.size - self.cut)
            self.down_far = send(high, high, moved(self.dim, -1))

        def end(self):
            arrived(self.up_far, window(self.piece(2), self.cut))
            arrived(self.down_far, window(self.piece(2) + self.cut, self.size - self.cut))

        def share(self, *bys):
            for by in bys:
                to_sibling(self.part, self.piece(by), self.size)

    first_rings, second_rings, third_rings = [], [], []
    for part in range(3):
        first, tiles, _, _ = PARTS[part]
        i1, i2, i3 = spot(part)
        first_rings.append(Ring(part, 0, lambda i, part=part, i2=i2, i3=i3: place(part, i3, i2, i, core),
                                tiles, tiles // 2))
        second_rings.append(Ring(part, 1, lambda i, part=part, i3=i3: place(part, i3, i, 0, core),
                                 4 * tiles, 2 * tiles))
        third_rings.append({
            by: Ring(part, 2, lambda i, part=part, i2=i2, by=by: place(part, i, mod(i2 + by, 4), 0, core),
                     4 * tiles, 2 * tiles)
            for by in (0, -1, 1, 2)
        })

    for part, ring in enumerate(first_rings):
        first, tiles, _, _ = PARTS[part]
        ring.start(density.at[pl.ds(first, tiles)])
    def find(s, _):
        b = block_list[s]
        j = b & 3
        bz = (b >> 2) & 3
        blo = (b >> 4) & 1
        bc = (b >> 5) & 1
        by = (b >> 6) & 3
        bx = ((b >> 8) & 1) * 2 + blo
        places = (
            (((bc * 4 + bz) * 4 + by) * 4 + bx) * 6,
            768 + (((bc * 4 + bx) * 4 + bz) * 4 + by) * 5 - 6,
            1408 + (((bc * 4 + by) * 4 + bx) * 4 + bz) * 5 - 11,
        )
        for r in range(4):
            t = j * 4 + r
            index[s * 4 + r] = t + jnp.where(t < 6, places[0], jnp.where(t < 11, places[1], places[2]))
        return 0

    for ring in first_rings:
        ring.middle()
    for ring in first_rings:
        ring.end()
    for copy in own_tiles:
        copy.wait()
    for part in range(3):
        second_rings[part].start()
        third_rings[part][0].start()
        second_rings[part].share(0)
    for part in range(3):
        second_rings[part].middle()
        third_rings[part][-1].start()
        third_rings[part][1].start()
        second_rings[part].share(-1, 1)
    for part in range(3):
        second_rings[part].end()
        third_rings[part][2].start()
        second_rings[part].share(2)
    metric_n = send(
        metric.at[pl.ds(pl.multiple_of(core * 640, 128), 384), :],
        mw.at[pl.ds(pl.multiple_of(896 - core * 896, 128), 384), :],
        ext,
    )
    lax.fori_loop(0, SLOTS, find, 0)
    for part in range(3):
        third_rings[part][0].middle()
        third_rings[part][0].share(-1, 1)
    for by in (-1, 1):
        for part in range(3):
            third_rings[part][by].middle()
            third_rings[part][by].share(-1, 1)
    for part in range(3):
        third_rings[part][0].end()
        third_rings[part][0].share(2)
    for part in range(3):
        third_rings[part][2].middle()
        third_rings[part][2].share(-1, 1)
    for by in (-1, 1):
        for part in range(3):
            third_rings[part][by].end()
            third_rings[part][by].share(2)
    for part in range(3):
        third_rings[part][2].end()
        third_rings[part][2].share(2)

    own_metric.wait()
    arrived(metric_n, mw.at[pl.ds(pl.multiple_of(core * 896, 128), 384), :])
    eye = (lax.broadcasted_iota(jnp.int32, (HB, HB), 0) == lax.broadcasted_iota(jnp.int32, (HB, HB), 1))
    low_ok = jnp.logical_or(aux > 0, core == 1)
    high_ok = jnp.logical_or(aux < 7, core == 0)
    zero_block = jnp.zeros((HB, HB), BF16)

    def build(i, _):
        for half in range(2):
            n = 2 * i + half
            rows = pl.ds(pl.multiple_of(n * HB, HB), HB)
            middle = mw[rows, HB:2 * HB]
            diag = jnp.sum(jnp.where(eye, middle, 0.0), axis=1, keepdims=True)
            keep = jnp.logical_and(jnp.logical_or(n > 2, low_ok), jnp.logical_or(n < 7, high_ok))
            scale = jnp.where(keep, -1.0 / diag, 0.0)
            for k in range(3):
                block = mw[rows, k * HB:(k + 1) * HB]
                if k == 1:
                    block = jnp.where(eye, 0.0, block)
                block = (block * scale).T
                high = block.astype(BF16)
                low = (block - high.astype(F32)).astype(BF16)
                at = (k + half) * HB
                wh[i, at:at + HB, half * HB:(half + 1) * HB] = high
                wl[i, at:at + HB, half * HB:(half + 1) * HB] = low
            at = (3 - 3 * half) * HB
            wh[i, at:at + HB, half * HB:(half + 1) * HB] = zero_block
            wl[i, at:at + HB, half * HB:(half + 1) * HB] = zero_block
        return 0

    lax.fori_loop(0, 5, build, 0)
    diag_rows = []
    for n in range(3, 7):
        middle = mw[n * HB:(n + 1) * HB, HB:2 * HB]
        diag_rows.append(jnp.sum(jnp.where(eye, middle, 0.0), axis=0, keepdims=True))
    diag_row = jnp.concatenate(diag_rows, axis=1)

    for n, ref in sib_waits:
        arrived(n, ref)

    lane = lax.broadcasted_iota(jnp.int32, (16, BS), 1)

    def pick(s, _):
        live = jnp.where(lane < block_sizes[s], 1.0, 0.0).astype(BF16)
        column = pl.ds(pl.multiple_of(s * BS, BS), BS)
        for r in range(4):
            picked[r * 16:(r + 1) * 16, column] = held[index[s * 4 + r]] * live
        return 0

    lax.fori_loop(0, SLOTS, pick, 0)

    for copy in slab_copies:
        copy.wait()

    def fit(out, half):
        columns = pl.ds(pl.multiple_of(half * HALF, HALF), HALF)

        def step(n, _):
            rows = pl.ds(pl.multiple_of(n * CHUNK, CHUNK), CHUNK)
            term = jnp.dot(picked[:, rows], slab_v[rows, columns], preferred_element_type=F32)

            @pl.when(n == 0)
            def _():
                out[...] = term

            @pl.when(n > 0)
            def _():
                out[...] += term

            return 0

        lax.fori_loop(0, NCHUNK, step, 0)

    fit(sib_acc.at[0], 1 - core)
    n = send(sib_acc.at[0], sib_acc.at[1], sibling)
    fit(acc, core)
    arrived(n, sib_acc.at[1])
    for q in range(8):
        fit_send[q] = acc[q * 8:(q + 1) * 8, :] + sib_acc[1, q * 8:(q + 1) * 8, :]
    waits = []
    for o in range(1, 8):
        to = mod(chip + o, 8)
        n = send(fit_send.at[to], fit_recv.at[o], chips[o - 1])
        waits.append((n, fit_recv.at[o]))
    total = fit_send[chip]
    for o, (n, ref) in enumerate(waits):
        arrived(n, ref)
        total = total + fit_recv[o + 1]

    own_u[...] = total / diag_row
    n_sib = send(own_u, halo.at[core], sibling)
    n_ext = send(own_u, halo.at[1 - core], ext)
    u0[:, HALF:2 * HALF] = own_u[...]
    arrived(n_sib, halo.at[1 - core])
    arrived(n_ext, halo.at[core])
    u0[:, :HALF] = jnp.where(low_ok, halo[0], 0.0)
    u0[:, 2 * HALF:] = jnp.where(high_ok, halo[1], 0.0)
    u[...] = u0[...]
    for pairs in ((0, 1, 2, 3, 4), (0, 1, 2, 3, 4), (1, 2, 3), (1, 2, 3)):
        values = u[...]
        high = values.astype(BF16)
        lh[0:8, :] = values
        lh[8:16, :] = values - high.astype(F32)
        for i in pairs:
            left = lh[:, i * 256:i * 256 + 512].astype(BF16)
            one = jnp.dot(left, wh[i], preferred_element_type=F32)
            two = jnp.dot(left, wl[i], preferred_element_type=F32)
            cols = slice((2 * i + 1) * HB, (2 * i + 3) * HB)
            u[:, cols] = u0[:, cols] + (one[0:8] + (one[8:16] + two[0:8]))

    call[core, chip] = u[:, HALF:2 * HALF]
    own_ref = call.at[core, chip]
    waits = []
    n_own = send(own_ref, own_ref, sibling)
    for o in range(1, 8):
        waits.append((send(own_ref, own_ref, chips[o - 1]), call.at[core, mod(chip - o, 8)]))
    shared = [(n_own, call.at[1 - core, chip])]
    for o, (n, ref) in enumerate(waits):
        arrived(n, ref)
        shared.append((send(ref, ref, sibling), call.at[1 - core, mod(chip - o - 1, 8)]))
    for n, ref in shared:
        arrived(n, ref)
    for half in range(2):
        for q in range(4):
            value = jnp.concatenate([call[half, 2 * q], call[half, 2 * q + 1]], axis=0)
            coeffs[q * 16:(q + 1) * 16, half * HALF:(half + 1) * HALF] = value
            cb[q * 16:(q + 1) * 16, half * HALF:(half + 1) * HALF] = value.astype(BF16)

    def coulomb_part(to, store):
        def dots(start, slots):
            rows = pl.ds(pl.multiple_of((to * OWN + start) * BS, BS), slots * BS)
            out = lax.dot_general(cb[...], slab_v[rows, :], (((1,), (1,)), ((), ())),
                                  preferred_element_type=F32)
            for k in range(slots):
                store(start + k, out[:, k * BS:(k + 1) * BS])

        def two(i, _):
            dots(2 * i, 2)
            return 0

        lax.fori_loop(0, OWN // 2, two, 0)
        dots(OWN - 1, 1)

    def into(ref, *terms):
        def store(i, value):
            for term in terms:
                value = value + term[i].astype(F32)
            ref[i] = value.astype(ref.dtype)
        return store

    up, down = moved(2, 1), moved(2, -1)
    z_up, z_down, z_far = mod(z + 1, 4), mod(z - 1, 4), mod(z + 2, 4)
    coulomb_part(z_far, into(opp_send.at[0]))
    n_a = send(opp_send.at[0], opp_recv.at[0], up)
    coulomb_part(4 + z_far, into(opp_send.at[1]))
    n_b = send(opp_send.at[1], opp_recv.at[1], down)
    waits = []

    def neighbour(to, k, into_store, target):
        coulomb_part(to, into_store)
        waits.append((send(nb_send.at[k], nb_recv.at[k], target), nb_recv.at[k]))

    neighbour(4 + z_up, 0, into(nb_send.at[0]), up)
    neighbour(z_down, 1, into(nb_send.at[1]), down)
    arrived(n_a, opp_recv.at[0])
    neighbour(z_up, 2, into(nb_send.at[2], opp_recv.at[0]), up)
    arrived(n_b, opp_recv.at[1])
    neighbour(4 + z_down, 3, into(nb_send.at[3], opp_recv.at[1]), down)
    lo = aux // 4
    other = 1 - lo
    coulomb_part(other * 4 + z, into(mine.at[1]))
    coulomb_part(lo * 4 + z, into(mine.at[0]))
    for n, ref in waits:
        arrived(n, ref)
    for i in range(OWN):
        value = mine[1, i] + nb_recv[2 - 2 * other, i].astype(F32) + nb_recv[1 + 2 * other, i].astype(F32)
        x_send[i] = value.astype(BF16)
    n_x = send(x_send, x_recv, x_mate)
    for i in range(OWN):
        mine[0, i] = mine[0, i] + nb_recv[2 - 2 * lo, i].astype(F32) + nb_recv[1 + 2 * lo, i].astype(F32)
    arrived(n_x, x_recv)
    row_lane = lax.broadcasted_iota(jnp.int32, (ND, BS), 1)
    for i in range(OWN):
        value = mine[0, i] + x_recv[i].astype(F32)
        live = row_lane < block_sizes[aux * OWN + i]
        coulomb[i] = jnp.where(live, value, 0.0).astype(BF16)

    for copy in sent:
        copy.wait_send()


NSEMS = 180


def shards(slab, density, block_list, block_sizes, metric):
    vmem = pl.BlockSpec(memory_space=pltpu.VMEM)
    smem = pl.BlockSpec(memory_space=pltpu.SMEM)
    hbm = pl.BlockSpec(memory_space=pl.ANY)
    coulomb, coeffs = pl.pallas_call(
        kernel,
        out_shape=(
            jax.ShapeDtypeStruct((OWN, ND, BS), BF16),
            jax.ShapeDtypeStruct((ND, AUX), F32),
        ),
        in_specs=[smem, smem, hbm, hbm, hbm],
        out_specs=(vmem, vmem),
        scratch_shapes=[
            pltpu.VMEM((ROWS, AUX), BF16),
            pltpu.VMEM((2048, 16, BS), BF16),
            pltpu.VMEM((ND, ROWS), BF16),
            pltpu.VMEM((ND, HALF), F32),
            pltpu.VMEM((2, ND, HALF), F32),
            pltpu.VMEM((8, 8, HALF), F32),
            pltpu.VMEM((8, 8, HALF), F32),
            pltpu.VMEM((1280, 3 * HB), F32),
            pltpu.VMEM((5, 512, 256), BF16),
            pltpu.VMEM((5, 512, 256), BF16),
            pltpu.VMEM((8, 3 * HALF), F32),
            pltpu.VMEM((8, 3 * HALF), F32),
            pltpu.VMEM((16, 3 * HALF), F32),
            pltpu.VMEM((8, HALF), F32),
            pltpu.VMEM((2, 8, HALF), F32),
            pltpu.VMEM((2, 8, 8, HALF), F32),
            pltpu.VMEM((ND, AUX), BF16),
            pltpu.VMEM((2, OWN, ND, BS), BF16),
            pltpu.VMEM((2, OWN, ND, BS), BF16),
            pltpu.VMEM((4, OWN, ND, BS), BF16),
            pltpu.VMEM((4, OWN, ND, BS), BF16),
            pltpu.VMEM((OWN, ND, BS), BF16),
            pltpu.VMEM((OWN, ND, BS), BF16),
            pltpu.VMEM((2, OWN, ND, BS), F32),
            pltpu.SMEM((4 * SLOTS,), jnp.int32),
            pltpu.SemaphoreType.DMA((NCHUNK,)),
            pltpu.SemaphoreType.DMA((4,)),
            pltpu.SemaphoreType.DMA((NSEMS,)),
            pltpu.SemaphoreType.DMA((NSEMS,)),
        ],
        compiler_params=pltpu.CompilerParams(
            collective_id=0, has_side_effects=True, vmem_limit_bytes=56 * 1024 * 1024
        ),
        cost_estimate=pl.CostEstimate(flops=4 * ND * ROWS * AUX, bytes_accessed=2 * ROWS * AUX, transcendentals=0),
    )(block_list, block_sizes, density.reshape(16, 16, BS), slab, metric)
    return coulomb, coeffs


def solution(mesh):
    return jax.shard_map(
        shards,
        mesh=mesh,
        in_specs=(
            P("pair", "aux"),
            P(("pair", "aux"), None, None),
            P("pair"),
            P("pair"),
            P("aux", None),
        ),
        out_specs=(P(("pair", "aux"), None, None), P(None, "aux")),
        check_vma=False,
    )
```

```python
import jax
import jax.numpy as jnp
from jax import lax
from jax.experimental import pallas as pl
from jax.experimental.pallas import tpu as pltpu
from jax.sharding import PartitionSpec as P

F32 = jnp.float32
BF16 = jnp.bfloat16
BS = 128
HB = 128
ND = 64
SLOTS = 88
OWN = 11
AUX = 1024
HALF = 512
ROWS = SLOTS * BS
XS = 5
ZS = OWN - XS
CHUNK = 1024
NCHUNK = ROWS // CHUNK

PARTS = (
    (0, 6, 0, (0, 1, 2)),
    (6, 5, 768, (1, 2, 0)),
    (11, 5, 1408, (2, 0, 1)),
)


def mod(value, size):
    return lax.rem(value + size, size)


def kernel(block_list, block_sizes, density, slab, metric, coulomb, coeffs, *scratch):
    (slab_v, held, picked, acc, sib_acc, fit_send, fit_recv, mw, wh, wl, u0, u, lh,
     own_u, halo, call, cb, zfar_send, zfar_recv, znb_send, znb_recv, zx_send, zx_recv, z_mine,
     xs_send, xs_recv, xfar_send, xfar_recv, xnb_send, xnb_recv, x_mine, index, slab_sem, local_sem, send_sem, recv_sem) = scratch

    pair = lax.axis_index("pair")
    aux = lax.axis_index("aux")
    core = lax.rem(pair, 2)
    chip = pair // 2
    x = (chip // 4) * 2 + aux // 4
    y = lax.rem(chip, 4)
    z = lax.rem(aux, 4)

    def device(coords, at_core):
        ax, ay, az = coords
        return (((ax // 2) * 4 + ay) * 2 + at_core, lax.rem(ax, 2) * 4 + az)

    moves = {}
    for dim in range(3):
        for by in (1, -1, 2):
            coords = [x, y, z]
            coords[dim] = mod(coords[dim] + by, 4)
            moves[dim, by] = device(coords, core)

    def moved(dim, by):
        return moves[dim, by]

    sibling = device([x, y, z], 1 - core)
    ext_aux = mod(aux + 2 * core - 1, 8)
    ext = (chip * 2 + (1 - core), ext_aux)
    chips = [(mod(chip + o, 8) * 2 + core, aux) for o in range(1, 8)]
    x_mate = (pair, mod(aux + 4, 8))

    barrier = pltpu.get_barrier_semaphore()
    partners = [moves[0, 1], moves[0, -1], moves[2, 1], moves[2, -1], moves[2, 2], sibling, ext]
    partners += chips + [(mod(chip + o, 8) * 2 + 1 - core, aux) for o in range(1, 8)]
    for partner in partners:
        pl.semaphore_signal(barrier, inc=1, device_id=partner, device_id_type=pl.DeviceIdType.MESH)

    slab_copies = []
    for n in range(NCHUNK):
        rows = pl.ds(n * CHUNK, CHUNK)
        slab_copies.append(pltpu.make_async_copy(slab.at[rows, :], slab_v.at[rows, :], slab_sem.at[n]))

    own_metric = pltpu.make_async_copy(
        metric.at[pl.ds(pl.multiple_of(core * 128, 128), 896), :],
        mw.at[pl.ds(pl.multiple_of(384 - core * 384, 128), 896), :],
        local_sem.at[0],
    )
    own_metric.start()

    def place(part, i3, i2, i1, at_core):
        _, tiles, base, _ = PARTS[part]
        return base + (((at_core * 4 + i3) * 4 + i2) * 4 + i1) * tiles

    def spot(part):
        order = PARTS[part][3]
        coords = (x, y, z)
        return coords[order[0]], coords[order[1]], coords[order[2]]

    own_tiles = []
    for part, (first, tiles, _, _) in enumerate(PARTS):
        i1, i2, i3 = spot(part)
        copy = pltpu.make_async_copy(
            density.at[pl.ds(first, tiles)],
            held.at[pl.ds(place(part, i3, i2, i1, core), tiles)],
            local_sem.at[1 + part],
        )
        copy.start()
        own_tiles.append(copy)

    pl.semaphore_wait(barrier, len(partners))
    for copy in own_tiles:
        copy.wait()

    count = [0]
    sent = []

    def send(src, dst, to):
        n = count[0]
        count[0] += 1
        copy = pltpu.make_async_remote_copy(
            src_ref=src, dst_ref=dst, send_sem=send_sem.at[n], recv_sem=recv_sem.at[n],
            device_id=to, device_id_type=pl.DeviceIdType.MESH,
        )
        copy.start()
        sent.append(copy)
        return n

    def arrived(n, ref):
        pltpu.make_async_remote_copy(
            src_ref=ref, dst_ref=ref, send_sem=send_sem.at[n], recv_sem=recv_sem.at[n],
            device_id=sibling, device_id_type=pl.DeviceIdType.MESH,
        ).wait_recv()

    def window(start, size):
        return held.at[pl.ds(start, size)]

    sib_waits = []

    def to_sibling(part, start, size):
        _, tiles, _, _ = PARTS[part]
        ref = window(start, size)
        n = send(ref, ref, sibling)
        other = start + (1 - 2 * core) * 64 * tiles
        sib_waits.append((n, window(other, size)))

    class Ring:
        def __init__(self, part, level, start_of, size, cut=0):
            self.part, self.start_of, self.size, self.cut = part, start_of, size, cut
            self.dim = PARTS[part][3][level]
            self.at = (x, y, z)[self.dim]

        def piece(self, by):
            return self.start_of(mod(self.at + by, 4))

        def start(self, src=None):
            ref = window(self.piece(0), self.size)
            src = ref if src is None else src
            self.up = send(src, ref, moved(self.dim, 1))
            self.down = send(src, ref, moved(self.dim, -1))
            if self.cut == 0:
                self.far = send(src, ref, moved(self.dim, 2))

        def middle(self):
            arrived(self.up, window(self.piece(-1), self.size))
            if self.cut == 0:
                arrived(self.down, window(self.piece(1), self.size))
                return
            low = window(self.piece(-1), self.cut)
            self.up_far = send(low, low, moved(self.dim, 1))
            arrived(self.down, window(self.piece(1), self.size))
            high = window(self.piece(1) + self.cut, self.size - self.cut)
            self.down_far = send(high, high, moved(self.dim, -1))

        def end(self):
            if self.cut == 0:
                arrived(self.far, window(self.piece(2), self.size))
                return
            arrived(self.up_far, window(self.piece(2), self.cut))
            arrived(self.down_far, window(self.piece(2) + self.cut, self.size - self.cut))

        def share(self, *bys):
            for by in bys:
                to_sibling(self.part, self.piece(by), self.size)

    first_rings, second_rings, third_rings = [], [], []
    for part in range(3):
        first, tiles, _, _ = PARTS[part]
        i1, i2, i3 = spot(part)
        first_rings.append(Ring(part, 0, lambda i, part=part, i2=i2, i3=i3: place(part, i3, i2, i, core),
                                tiles))
        second_rings.append(Ring(part, 1, lambda i, part=part, i3=i3: place(part, i3, i, 0, core),
                                 4 * tiles))
        third_rings.append({
            by: Ring(part, 2, lambda i, part=part, i2=i2, by=by: place(part, i, mod(i2 + by, 4), 0, core),
                     4 * tiles, 2 * tiles)
            for by in (0, -1, 1, 2)
        })

    for part, ring in enumerate(first_rings):
        first, tiles, _, _ = PARTS[part]
        ring.start()
    for copy in slab_copies:
        copy.start()

    def find(s, _):
        b = block_list[s]
        j = b & 3
        bz = (b >> 2) & 3
        blo = (b >> 4) & 1
        bc = (b >> 5) & 1
        by = (b >> 6) & 3
        bx = ((b >> 8) & 1) * 2 + blo
        places = (
            (((bc * 4 + bz) * 4 + by) * 4 + bx) * 6,
            768 + (((bc * 4 + bx) * 4 + bz) * 4 + by) * 5 - 6,
            1408 + (((bc * 4 + by) * 4 + bx) * 4 + bz) * 5 - 11,
        )
        for r in range(4):
            t = j * 4 + r
            index[s * 4 + r] = t + jnp.where(t < 6, places[0], jnp.where(t < 11, places[1], places[2]))
        return 0

    for ring in first_rings:
        ring.middle()
    for ring in first_rings:
        ring.end()
    for part in range(3):
        second_rings[part].start()
    for part in range(3):
        third_rings[part][0].start()
    for part in range(3):
        second_rings[part].share(0)
    for part in range(3):
        second_rings[part].middle()
    for part in range(3):
        third_rings[part][-1].start()
        third_rings[part][1].start()
    for part in range(3):
        second_rings[part].share(-1, 1)
    for part in range(3):
        second_rings[part].end()
    for part in range(3):
        third_rings[part][2].start()
    for part in range(3):
        second_rings[part].share(2)
    lax.fori_loop(0, SLOTS, find, 0)
    eye = (lax.broadcasted_iota(jnp.int32, (HB, HB), 0) == lax.broadcasted_iota(jnp.int32, (HB, HB), 1))
    low_ok = jnp.logical_or(aux > 0, core == 1)
    high_ok = jnp.logical_or(aux < 7, core == 0)
    zero_block = jnp.zeros((HB, HB), BF16)

    def build(i):
        for half in range(2):
            n = 2 * i + half
            rows = pl.ds(pl.multiple_of(n * HB, HB), HB)
            middle = mw[rows, HB:2 * HB]
            diag = jnp.sum(jnp.where(eye, middle, 0.0), axis=1, keepdims=True)
            keep = jnp.logical_and(jnp.logical_or(n > 2, low_ok), jnp.logical_or(n < 7, high_ok))
            scale = jnp.where(keep, -1.0 / diag, 0.0)
            for k in range(3):
                block = mw[rows, k * HB:(k + 1) * HB]
                if k == 1:
                    block = jnp.where(eye, 0.0, block)
                block = (block * scale).T
                high = block.astype(BF16)
                low = (block - high.astype(F32)).astype(BF16)
                at = (k + half) * HB
                wh[i, at:at + HB, half * HB:(half + 1) * HB] = high
                wl[i, at:at + HB, half * HB:(half + 1) * HB] = low
            at = (3 - 3 * half) * HB
            wh[i, at:at + HB, half * HB:(half + 1) * HB] = zero_block
            wl[i, at:at + HB, half * HB:(half + 1) * HB] = zero_block
        return 0


    for by in (0, -1, 1, 2):
        for part in range(3):
            third_rings[part][by].middle()
        for part in range(3):
            third_rings[part][by].share(-1, 1)
    own_metric.wait()
    lax.fori_loop(0, 3, lambda i, _: build(2 - 2 * core + i), 0)
    diag_rows = []
    for n in range(3, 7):
        middle = mw[n * HB:(n + 1) * HB, HB:2 * HB]
        diag_rows.append(jnp.sum(jnp.where(eye, middle, 0.0), axis=0, keepdims=True))
    diag_row = jnp.concatenate(diag_rows, axis=1)
    for by in (0, -1, 1, 2):
        for part in range(3):
            third_rings[part][by].end()
        for part in range(3):
            third_rings[part][by].share(2)
    metric_n = send(
        metric.at[pl.ds(pl.multiple_of(core * 640, 128), 384), :],
        mw.at[pl.ds(pl.multiple_of(896 - core * 896, 128), 384), :],
        ext,
    )

    for n, ref in sib_waits:
        arrived(n, ref)

    lane = lax.broadcasted_iota(jnp.int32, (16, BS), 1)

    def pick(s, _):
        live = jnp.where(lane < block_sizes[s], 1.0, 0.0).astype(BF16)
        column = pl.ds(pl.multiple_of(s * BS, BS), BS)
        for r in range(4):
            picked[r * 16:(r + 1) * 16, column] = held[index[s * 4 + r]] * live
        return 0

    lax.fori_loop(0, SLOTS, pick, 0)

    for copy in slab_copies:
        copy.wait()

    def fit(out, half):
        def step(n, _):
            columns = pl.ds(pl.multiple_of(half * HALF + n * 256, 256), 256)
            out[n] = jnp.dot(picked[...], slab_v[:, columns], preferred_element_type=F32)
            return 0

        lax.fori_loop(0, 2, step, 0)

    fit(sib_acc.at[0], 1 - core)
    n = send(sib_acc.at[0], sib_acc.at[1], sibling)
    fit(acc, core)
    arrived(n, sib_acc.at[1])
    for q in range(8):
        for n in range(2):
            rows = slice(q * 8, (q + 1) * 8)
            fit_send[q, :, n * 256:(n + 1) * 256] = acc[n, rows, :] + sib_acc[1, n, rows, :]
    waits = []
    for o in range(1, 8):
        to = mod(chip + o, 8)
        n = send(fit_send.at[to], fit_recv.at[o], chips[o - 1])
        waits.append((n, fit_recv.at[o]))
    arrived(metric_n, mw.at[pl.ds(pl.multiple_of(core * 896, 128), 384), :])
    lax.fori_loop(0, 2, lambda i, _: build(3 * core + i), 0)
    total = fit_send[chip]
    for o, (n, ref) in enumerate(waits):
        arrived(n, ref)
        total = total + fit_recv[o + 1]

    own_u[...] = total / diag_row
    n_sib = send(own_u, halo.at[core], sibling)
    n_ext = send(own_u, halo.at[1 - core], ext)
    u0[:, HALF:2 * HALF] = own_u[...]
    arrived(n_sib, halo.at[1 - core])
    arrived(n_ext, halo.at[core])
    u0[:, :HALF] = jnp.where(low_ok, halo[0], 0.0)
    u0[:, 2 * HALF:] = jnp.where(high_ok, halo[1], 0.0)
    u[...] = u0[...]
    for pairs in ((0, 1, 2, 3, 4), (0, 1, 2, 3, 4), (1, 2, 3), (1, 2, 3)):
        values = u[...]
        high = values.astype(BF16)
        lh[0:8, :] = values
        lh[8:16, :] = values - high.astype(F32)
        for i in pairs:
            left = lh[:, i * 256:i * 256 + 512].astype(BF16)
            one = jnp.dot(left, wh[i], preferred_element_type=F32)
            two = jnp.dot(left, wl[i], preferred_element_type=F32)
            cols = slice((2 * i + 1) * HB, (2 * i + 3) * HB)
            u[:, cols] = u0[:, cols] + (one[0:8] + (one[8:16] + two[0:8]))

    call[core, chip] = u[:, HALF:2 * HALF]
    own_ref = call.at[core, chip]
    waits = []
    for o in range(1, 8):
        other = (mod(chip + o, 8) * 2 + 1 - core, aux)
        waits.append((send(own_ref, own_ref, chips[o - 1]), call.at[core, mod(chip - o, 8)]))
        waits.append((send(own_ref, own_ref, other), call.at[1 - core, mod(chip - o, 8)]))
    waits.append((send(own_ref, own_ref, sibling), call.at[1 - core, chip]))
    for n, ref in waits:
        arrived(n, ref)
    for half in range(2):
        for q in range(4):
            value = jnp.concatenate([call[half, 2 * q], call[half, 2 * q + 1]], axis=0)
            coeffs[q * 16:(q + 1) * 16, half * HALF:(half + 1) * HALF] = value
            cb[q * 16:(q + 1) * 16, half * HALF:(half + 1) * HALF] = value.astype(BF16)

    def dots(to, start, slots):
        rows = pl.ds(pl.multiple_of(to * (OWN * BS) + start * BS, BS), slots * BS)
        return lax.dot_general(cb[...], slab_v[rows, :], (((1,), (1,)), ((), ())),
                               preferred_element_type=F32)

    def put(ref, value, *terms):
        slots = value.shape[1] // BS
        for k in range(slots):
            part = value[:, k * BS:(k + 1) * BS]
            for term, first in terms:
                if first <= k < first + term.shape[0]:
                    part = part + term[k - first].astype(F32)
            ref[k] = part.astype(ref.dtype)

    def z_part(to):
        return dots(to, XS, ZS)

    def x_part(to):
        return dots(to, 0, XS)

    up, down = moved(2, 1), moved(2, -1)
    z_up, z_down, z_far = mod(z + 1, 4), mod(z - 1, 4), mod(z + 2, 4)
    lo = aux // 4
    other = 1 - lo

    put(zfar_send.at[0], z_part(z_far))
    n_zfar0 = send(zfar_send.at[0], zfar_recv.at[0], up)
    put(zfar_send.at[1], z_part(4 + z_far))
    n_zfar1 = send(zfar_send.at[1], zfar_recv.at[1], down)
    put(xs_send.at[0], x_part(other * 4 + z_far))
    n_xs0 = send(xs_send.at[0], xs_recv.at[0], x_mate)
    put(znb_send.at[0], z_part(4 + z_up))
    n_znb0 = send(znb_send.at[0], znb_recv.at[0], up)
    put(znb_send.at[1], z_part(z_down))
    n_znb1 = send(znb_send.at[1], znb_recv.at[1], down)
    put(xs_send.at[1], x_part(other * 4 + z_up))
    n_xs1 = send(xs_send.at[1], xs_recv.at[1], x_mate)
    put(xs_send.at[2], x_part(other * 4 + z_down))
    n_xs2 = send(xs_send.at[2], xs_recv.at[2], x_mate)

    arrived(n_xs0, xs_recv.at[0])
    put(xfar_send, x_part(lo * 4 + z_far), (xs_recv.at[0], 0))
    first, second = pl.ds(0, 2), pl.ds(2, XS - 2)
    n_xfar0 = send(xfar_send.at[first], xfar_recv.at[first], up)
    n_xfar1 = send(xfar_send.at[second], xfar_recv.at[second], down)
    arrived(n_zfar0, zfar_recv.at[0])
    put(znb_send.at[2], z_part(z_up), (zfar_recv.at[0], 0))
    n_znb2 = send(znb_send.at[2], znb_recv.at[2], up)
    arrived(n_zfar1, zfar_recv.at[1])
    put(znb_send.at[3], z_part(4 + z_down), (zfar_recv.at[1], 0))
    n_znb3 = send(znb_send.at[3], znb_recv.at[3], down)
    put(xs_send.at[3], x_part(other * 4 + z))
    n_xs3 = send(xs_send.at[3], xs_recv.at[3], x_mate)
    put(z_mine.at[1], z_part(other * 4 + z))
    arrived(n_xs1, xs_recv.at[1])
    arrived(n_xfar0, xfar_recv.at[first])
    put(xnb_send.at[0], x_part(lo * 4 + z_up), (xs_recv.at[1], 0), (xfar_recv.at[first], 0))
    n_xnb0 = send(xnb_send.at[0], xnb_recv.at[0], up)
    arrived(n_xs2, xs_recv.at[2])
    arrived(n_xfar1, xfar_recv.at[second])
    put(xnb_send.at[1], x_part(lo * 4 + z_down), (xs_recv.at[2], 0), (xfar_recv.at[second], 2))
    n_xnb1 = send(xnb_send.at[1], xnb_recv.at[1], down)
    put(z_mine.at[0], z_part(lo * 4 + z))
    put(x_mine, x_part(lo * 4 + z))

    for k, n in enumerate((n_znb0, n_znb1, n_znb2, n_znb3)):
        arrived(n, znb_recv.at[k])

    def z_sum(k, which, i):
        return (z_mine[k, i] + znb_recv[2 - 2 * which, i].astype(F32)
                + znb_recv[1 + 2 * which, i].astype(F32))

    for i in range(ZS):
        zx_send[i] = z_sum(1, other, i).astype(BF16)
    n_zx = send(zx_send, zx_recv, x_mate)

    row_lane = lax.broadcasted_iota(jnp.int32, (ND, BS), 1)

    def finish(i, value):
        live = row_lane < block_sizes[aux * OWN + i]
        coulomb[i] = jnp.where(live, value, 0.0).astype(BF16)

    for i in range(ZS):
        z_mine[0, i] = z_sum(0, lo, i)
    arrived(n_xs3, xs_recv.at[3])
    arrived(n_xnb0, xnb_recv.at[0])
    arrived(n_xnb1, xnb_recv.at[1])
    for i in range(XS):
        finish(i, x_mine[i] + xs_recv[3, i].astype(F32) + xnb_recv[0, i].astype(F32)
               + xnb_recv[1, i].astype(F32))
    arrived(n_zx, zx_recv)
    for i in range(ZS):
        finish(XS + i, z_mine[0, i] + zx_recv[i].astype(F32))

    for copy in sent:
        copy.wait_send()


NSEMS = 180


def shards(slab, density, block_list, block_sizes, metric):
    vmem = pl.BlockSpec(memory_space=pltpu.VMEM)
    smem = pl.BlockSpec(memory_space=pltpu.SMEM)
    hbm = pl.BlockSpec(memory_space=pl.ANY)
    coulomb, coeffs = pl.pallas_call(
        kernel,
        out_shape=(
            jax.ShapeDtypeStruct((OWN, ND, BS), BF16),
            jax.ShapeDtypeStruct((ND, AUX), F32),
        ),
        in_specs=[smem, smem, hbm, hbm, hbm],
        out_specs=(vmem, vmem),
        scratch_shapes=[
            pltpu.VMEM((ROWS, AUX), BF16),
            pltpu.VMEM((2048, 16, BS), BF16),
            pltpu.VMEM((ND, ROWS), BF16),
            pltpu.VMEM((2, ND, 256), F32),
            pltpu.VMEM((2, 2, ND, 256), F32),
            pltpu.VMEM((8, 8, HALF), F32),
            pltpu.VMEM((8, 8, HALF), F32),
            pltpu.VMEM((1280, 3 * HB), F32),
            pltpu.VMEM((5, 512, 256), BF16),
            pltpu.VMEM((5, 512, 256), BF16),
            pltpu.VMEM((8, 3 * HALF), F32),
            pltpu.VMEM((8, 3 * HALF), F32),
            pltpu.VMEM((16, 3 * HALF), F32),
            pltpu.VMEM((8, HALF), F32),
            pltpu.VMEM((2, 8, HALF), F32),
            pltpu.VMEM((2, 8, 8, HALF), F32),
            pltpu.VMEM((ND, AUX), BF16),
            pltpu.VMEM((2, ZS, ND, BS), BF16),
            pltpu.VMEM((2, ZS, ND, BS), BF16),
            pltpu.VMEM((4, ZS, ND, BS), BF16),
            pltpu.VMEM((4, ZS, ND, BS), BF16),
            pltpu.VMEM((ZS, ND, BS), BF16),
            pltpu.VMEM((ZS, ND, BS), BF16),
            pltpu.VMEM((2, ZS, ND, BS), F32),
            pltpu.VMEM((4, XS, ND, BS), BF16),
            pltpu.VMEM((4, XS, ND, BS), BF16),
            pltpu.VMEM((XS, ND, BS), BF16),
            pltpu.VMEM((XS, ND, BS), BF16),
            pltpu.VMEM((2, XS, ND, BS), BF16),
            pltpu.VMEM((2, XS, ND, BS), BF16),
            pltpu.VMEM((XS, ND, BS), F32),
            pltpu.SMEM((4 * SLOTS,), jnp.int32),
            pltpu.SemaphoreType.DMA((NCHUNK,)),
            pltpu.SemaphoreType.DMA((4,)),
            pltpu.SemaphoreType.DMA((NSEMS,)),
            pltpu.SemaphoreType.DMA((NSEMS,)),
        ],
        compiler_params=pltpu.CompilerParams(
            collective_id=0, has_side_effects=True, vmem_limit_bytes=56 * 1024 * 1024
        ),
        cost_estimate=pl.CostEstimate(flops=4 * ND * ROWS * AUX, bytes_accessed=2 * ROWS * AUX, transcendentals=0),
    )(block_list, block_sizes, density.reshape(16, 16, BS), slab, metric)
    return coulomb, coeffs


def solution(mesh):
    return jax.shard_map(
        shards,
        mesh=mesh,
        in_specs=(
            P("pair", "aux"),
            P(("pair", "aux"), None, None),
            P("pair"),
            P("pair"),
            P("aux", None),
        ),
        out_specs=(P(("pair", "aux"), None, None), P(None, "aux")),
        check_vma=False,
    )
```

```python
import jax
import jax.numpy as jnp
from jax import lax
from jax.experimental import pallas as pl
from jax.experimental.pallas import tpu as pltpu
from jax.sharding import PartitionSpec as P

F32 = jnp.float32
BF16 = jnp.bfloat16
BS = 128
HB = 128
ND = 64
SLOTS = 88
OWN = 11
AUX = 1024
HALF = 512
ROWS = SLOTS * BS
XS = 5
ZS = OWN - XS
CHUNK = 1024
NCHUNK = ROWS // CHUNK

PARTS = (
    (0, 5, 0, (0, 1, 2)),
    (5, 5, 640, (1, 2, 0)),
    (10, 6, 1280, (2, 0, 1)),
)


def mod(value, size):
    return lax.rem(value + size, size)


def kernel(block_list, block_sizes, density, slab, metric, coulomb, coeffs, *scratch):
    (slab_v, held, picked, acc, sib_acc, fit_send, fit_recv, mw, wh, wl, u0, u, lh,
     own_u, halo, call, rounded, cb, z_wait, zfar_send, zfar_recv, znb_send, znb_recv, zx_send, zx_recv, z_mine,
     xs_send, xs_recv, xfar_send, xfar_recv, xnb_send, xnb_recv, x_mine, index, slab_sem, local_sem, send_sem, recv_sem) = scratch

    pair = lax.axis_index("pair")
    aux = lax.axis_index("aux")
    core = lax.rem(pair, 2)
    chip = pair // 2
    x = (chip // 4) * 2 + aux // 4
    y = lax.rem(chip, 4)
    z = lax.rem(aux, 4)

    def device(coords, at_core):
        ax, ay, az = coords
        return (((ax // 2) * 4 + ay) * 2 + at_core, lax.rem(ax, 2) * 4 + az)

    moves = {}
    for dim in range(3):
        for by in (1, -1, 2):
            coords = [x, y, z]
            coords[dim] = mod(coords[dim] + by, 4)
            moves[dim, by] = device(coords, core)

    def moved(dim, by):
        return moves[dim, by]

    sibling = device([x, y, z], 1 - core)
    ext_aux = mod(aux + 2 * core - 1, 8)
    ext = (chip * 2 + (1 - core), ext_aux)
    steps = ((1, 2), (1, 1), (1, 3), (1, 0), (0, 2), (0, 1), (0, 3))
    chip_to = [mod(chip // 4 + flip, 2) * 4 + mod(y + by, 4) for flip, by in steps]
    chip_from = [mod(chip // 4 + flip, 2) * 4 + mod(y - by, 4) for flip, by in steps]
    chips = [(to * 2 + core, aux) for to in chip_to]
    other_cores = [(to * 2 + 1 - core, aux) for to in chip_to]
    x_mate = (pair, mod(aux + 4, 8))

    barrier = pltpu.get_barrier_semaphore()
    partners = chips + other_cores
    partners += [ext, moves[2, 2], moves[0, 1], moves[0, -1], moves[2, 1], moves[2, -1], sibling]
    for partner in partners:
        pl.semaphore_signal(barrier, inc=1, device_id=partner, device_id_type=pl.DeviceIdType.MESH)

    slab_copies = []
    for n in range(NCHUNK):
        rows = pl.ds(n * CHUNK, CHUNK)
        slab_copies.append(pltpu.make_async_copy(slab.at[rows, :], slab_v.at[rows, :], slab_sem.at[n]))

    own_metric = pltpu.make_async_copy(
        metric.at[pl.ds(pl.multiple_of(core * 128, 128), 896), :],
        mw.at[pl.ds(pl.multiple_of(384 - core * 384, 128), 896), :],
        local_sem.at[0],
    )
    own_metric.start()

    def place(part, far3=0, far2=0, far1=0):
        _, tiles, base, _ = PARTS[part]
        return base + core * (64 * tiles) + ((far3 * 4 + far2) * 4 + far1) * tiles

    own_tiles = []
    for part, (first, tiles, _, _) in enumerate(PARTS):
        copy = pltpu.make_async_copy(
            density.at[pl.ds(first, tiles)],
            held.at[pl.ds(place(part), tiles)],
            local_sem.at[1 + part],
        )
        copy.start()
        own_tiles.append(copy)

    pl.semaphore_wait(barrier, len(partners))
    for copy in own_tiles:
        copy.wait()

    count = [0]
    sent = []

    def send(src, dst, to):
        n = count[0]
        count[0] += 1
        copy = pltpu.make_async_remote_copy(
            src_ref=src, dst_ref=dst, send_sem=send_sem.at[n], recv_sem=recv_sem.at[n],
            device_id=to, device_id_type=pl.DeviceIdType.MESH,
        )
        copy.start()
        sent.append(copy)
        return n

    def arrived(n, ref):
        pltpu.make_async_remote_copy(
            src_ref=ref, dst_ref=ref, send_sem=send_sem.at[n], recv_sem=recv_sem.at[n],
            device_id=sibling, device_id_type=pl.DeviceIdType.MESH,
        ).wait_recv()

    def window(start, size):
        return held.at[pl.ds(start, size)]

    sib_waits = []

    def to_sibling(part, start, size):
        _, tiles, _, _ = PARTS[part]
        ref = window(start, size)
        n = send(ref, ref, sibling)
        other = start + (1 - 2 * core) * 64 * tiles
        sib_waits.append((n, window(other, size)))

    class Ring:
        def __init__(self, part, level, first, tiles, cut=0):
            self.part, self.first, self.size = part, first, tiles
            self.cut = cut
            self.dim = PARTS[part][3][level]
            self.stride = PARTS[part][1] * 4 ** level

        def piece(self, far, start=0, size=None):
            return window(self.first + far * self.stride + start, self.size if size is None else size)

        def start(self):
            self.up = send(self.piece(0), self.piece(3), moved(self.dim, 1))
            self.down = send(self.piece(0), self.piece(1), moved(self.dim, -1))
            if self.cut == 0:
                self.far = send(self.piece(0), self.piece(2), moved(self.dim, 2))

        def middle(self):
            arrived(self.up, self.piece(3))
            if self.cut:
                self.up_far = send(self.piece(3, 0, self.cut), self.piece(2, 0, self.cut), moved(self.dim, 1))
            arrived(self.down, self.piece(1))
            if self.cut:
                rest = self.size - self.cut
                self.down_far = send(self.piece(1, self.cut, rest), self.piece(2, self.cut, rest),
                                     moved(self.dim, -1))

        def end(self):
            if self.cut == 0:
                arrived(self.far, self.piece(2))
                return
            arrived(self.up_far, self.piece(2, 0, self.cut))
            arrived(self.down_far, self.piece(2, self.cut, self.size - self.cut))

    def every(make):
        return [make(part, PARTS[part][1]) for part in range(3)]

    first_rings = every(lambda part, t: Ring(part, 0, place(part), t))
    second_own = every(lambda part, t: Ring(part, 1, place(part), t))
    second_rest = every(lambda part, t: Ring(part, 1, place(part) + t, 3 * t))
    third_own = every(lambda part, t: Ring(part, 2, place(part), t, t // 2))
    third_rest = every(lambda part, t: Ring(part, 2, place(part) + t, 3 * t, 3 * t // 2))
    third_rows = [None] + [
        every(lambda part, t, far=far: Ring(part, 2, place(part, 0, far), 4 * t, 2 * t)) for far in (1, 2, 3)
    ]

    def share(far3, far2, rows=1):
        for part in range(3):
            to_sibling(part, place(part, far3, far2), 4 * rows * PARTS[part][1])

    for ring in first_rings + second_own + third_own:
        ring.start()
    for copy in slab_copies:
        copy.start()

    def send_metric(start, rows):
        src = pl.multiple_of(core * 640 + start, 128)
        dst = pl.multiple_of(896 - core * 896 + start, 128)
        here = pl.multiple_of(core * 896 + start, 128)
        n = send(metric.at[pl.ds(src, rows), :], mw.at[pl.ds(dst, rows), :], ext)
        return n, mw.at[pl.ds(here, rows), :]

    metric_waits = [send_metric(0, 128)]

    def find(s, _):
        b = block_list[s]
        j = b & 3
        bz = (b >> 2) & 3
        blo = (b >> 4) & 1
        bc = (b >> 5) & 1
        by = (b >> 6) & 3
        bx = ((b >> 8) & 1) * 2 + blo
        bx, by, bz = (bx - x) & 3, (by - y) & 3, (bz - z) & 3
        places = (
            (((bc * 4 + bz) * 4 + by) * 4 + bx) * 5,
            640 + (((bc * 4 + bx) * 4 + bz) * 4 + by) * 5 - 5,
            1280 + (((bc * 4 + by) * 4 + bx) * 4 + bz) * 6 - 10,
        )
        for r in range(4):
            t = j * 4 + r
            index[s * 4 + r] = t + jnp.where(t < 5, places[0], jnp.where(t < 10, places[1], places[2]))
        return 0

    for ring in first_rings:
        ring.middle()
    for ring in first_rings:
        ring.end()
    for ring in second_rest + third_rest:
        ring.start()
    share(0, 0)
    for ring in third_own + second_own:
        ring.middle()
    for ring in second_rest:
        ring.middle()
    for ring in third_rows[3] + third_rows[1]:
        ring.start()
    share(0, 3)
    share(0, 1)
    for ring in second_own + second_rest:
        ring.end()
    for ring in third_rows[2]:
        ring.start()
    share(0, 2)
    lax.fori_loop(0, SLOTS, find, 0)
    eye = (lax.broadcasted_iota(jnp.int32, (HB, HB), 0) == lax.broadcasted_iota(jnp.int32, (HB, HB), 1))
    low_ok = jnp.logical_or(aux > 0, core == 1)
    high_ok = jnp.logical_or(aux < 7, core == 0)
    zero_block = jnp.zeros((HB, HB), BF16)

    def build(i):
        for half in range(2):
            n = 2 * i + half
            rows = pl.ds(pl.multiple_of(n * HB, HB), HB)
            middle = mw[rows, HB:2 * HB]
            diag = jnp.sum(jnp.where(eye, middle, 0.0), axis=1, keepdims=True)
            keep = jnp.logical_and(jnp.logical_or(n > 2, low_ok), jnp.logical_or(n < 7, high_ok))
            scale = jnp.where(keep, -1.0 / diag, 0.0)
            for k in range(3):
                block = mw[rows, k * HB:(k + 1) * HB]
                if k == 1:
                    block = jnp.where(eye, 0.0, block)
                block = (block * scale).T
                high = block.astype(BF16)
                low = (block - high.astype(F32)).astype(BF16)
                at = (k + half) * HB
                wh[i, at:at + HB, half * HB:(half + 1) * HB] = high
                wl[i, at:at + HB, half * HB:(half + 1) * HB] = low
            at = (3 - 3 * half) * HB
            wh[i, at:at + HB, half * HB:(half + 1) * HB] = zero_block
            wl[i, at:at + HB, half * HB:(half + 1) * HB] = zero_block
        return 0


    for ring in third_rest:
        ring.middle()
    share(3, 0)
    share(1, 0)
    for far in (3, 1, 2):
        for ring in third_rows[far]:
            ring.middle()
        share(3, far)
        share(1, far)
    metric_waits.append(send_metric(128, 256))
    own_metric.wait()
    lax.fori_loop(0, 3, lambda i, _: build(2 - 2 * core + i), 0)
    diag_rows = []
    for n in range(3, 7):
        middle = mw[n * HB:(n + 1) * HB, HB:2 * HB]
        diag_rows.append(jnp.sum(jnp.where(eye, middle, 0.0), axis=0, keepdims=True))
    diag_row = jnp.concatenate(diag_rows, axis=1)
    for ring in third_own + third_rest:
        ring.end()
    share(2, 0)
    for far in (3, 1, 2):
        for ring in third_rows[far]:
            ring.end()
        share(2, far)
    for n, ref in sib_waits:
        arrived(n, ref)

    lane = lax.broadcasted_iota(jnp.int32, (16, BS), 1)

    def pick(s, _):
        live = jnp.where(lane < block_sizes[s], 1.0, 0.0).astype(BF16)
        column = pl.ds(pl.multiple_of(s * BS, BS), BS)
        for r in range(4):
            picked[r * 16:(r + 1) * 16, column] = held[index[s * 4 + r]] * live
        return 0

    lax.fori_loop(0, SLOTS, pick, 0)

    for copy in slab_copies:
        copy.wait()

    def fit(out, half):
        def step(n, _):
            columns = pl.ds(pl.multiple_of(half * HALF + n * 256, 256), 256)
            out[n] = jnp.dot(picked[...], slab_v[:, columns], preferred_element_type=F32)
            return 0

        lax.fori_loop(0, 2, step, 0)

    fit(sib_acc.at[0], 1 - core)
    n = send(sib_acc.at[0], sib_acc.at[1], sibling)
    fit(acc, core)
    arrived(n, sib_acc.at[1])
    for q in range(8):
        for n in range(2):
            rows = slice(q * 8, (q + 1) * 8)
            fit_send[q, :, n * 256:(n + 1) * 256] = acc[n, rows, :] + sib_acc[1, n, rows, :]
    waits = []
    for o, to in enumerate(chip_to):
        n = send(fit_send.at[to], fit_recv.at[o], chips[o])
        waits.append((n, fit_recv.at[o]))
    for n, ref in metric_waits:
        arrived(n, ref)
    lax.fori_loop(0, 2, lambda i, _: build(3 * core + i), 0)
    total = fit_send[chip]
    for o, (n, ref) in enumerate(waits):
        arrived(n, ref)
        total = total + fit_recv[o]

    own_u[...] = total / diag_row
    n_sib = send(own_u, halo.at[core], sibling)
    n_ext = send(own_u, halo.at[1 - core], ext)
    u0[:, HALF:2 * HALF] = own_u[...]
    arrived(n_sib, halo.at[1 - core])
    arrived(n_ext, halo.at[core])
    u0[:, :HALF] = jnp.where(low_ok, halo[0], 0.0)
    u0[:, 2 * HALF:] = jnp.where(high_ok, halo[1], 0.0)
    u[...] = u0[...]
    for pairs in ((0, 1, 2, 3, 4), (0, 1, 2, 3, 4), (1, 2, 3), (1, 2, 3)):
        values = u[...]
        high = values.astype(BF16)
        lh[0:8, :] = values
        lh[8:16, :] = values - high.astype(F32)
        for i in pairs:
            left = lh[:, i * 256:i * 256 + 512].astype(BF16)
            one = jnp.dot(left, wh[i], preferred_element_type=F32)
            two = jnp.dot(left, wl[i], preferred_element_type=F32)
            cols = slice((2 * i + 1) * HB, (2 * i + 3) * HB)
            u[:, cols] = u0[:, cols] + (one[0:8] + (one[8:16] + two[0:8]))

    own = u[:, HALF:2 * HALF]
    call[core, chip] = own
    rounded[core, chip] = jnp.concatenate([own[:, :256], own[:, 256:]], axis=0).astype(BF16)
    ref = rounded.at[core, chip]
    waits = []
    for o, source in enumerate(chip_from):
        waits.append((send(ref, ref, chips[o]), rounded.at[core, source]))
        waits.append((send(ref, ref, other_cores[o]), rounded.at[1 - core, source]))
    waits.append((send(ref, ref, sibling), rounded.at[1 - core, chip]))
    ref = call.at[core, chip]
    full_waits = [(send(ref, ref, chips[o]), call.at[core, source]) for o, source in enumerate(chip_from)]
    for n, ref in waits:
        arrived(n, ref)
    for half in range(2):
        for q in range(4):
            two = [rounded[half, 2 * q + k].astype(F32) for k in range(2)]
            for k in range(2):
                part = slice(k * 8, (k + 1) * 8)
                cb[q * 16:(q + 1) * 16, half * HALF + k * 256:half * HALF + (k + 1) * 256] = (
                    jnp.concatenate([two[0][part], two[1][part]], axis=0).astype(BF16))

    def dots(to, start, slots):
        rows = pl.ds(pl.multiple_of(to * (OWN * BS) + start * BS, BS), slots * BS)
        return lax.dot_general(cb[...], slab_v[rows, :], (((1,), (1,)), ((), ())),
                               preferred_element_type=F32)

    def put(ref, value, *terms):
        slots = value.shape[1] // BS
        for k in range(slots):
            part = value[:, k * BS:(k + 1) * BS]
            for term, first in terms:
                if first <= k < first + term.shape[0]:
                    part = part + term[k - first].astype(F32)
            ref[k] = part.astype(ref.dtype)

    def z_part(to):
        return dots(to, XS, ZS)

    def x_part(to):
        return dots(to, 0, XS)

    up, down = moved(2, 1), moved(2, -1)
    z_up, z_down, z_far = mod(z + 1, 4), mod(z - 1, 4), mod(z + 2, 4)
    lo = aux // 4
    other = 1 - lo

    thirds = (pl.ds(0, 3), pl.ds(3, ZS - 3))

    def send_two(src, dst, to):
        return [(send(src.at[part], dst.at[part], to), dst.at[part]) for part in thirds]

    put(zfar_send.at[0], z_part(z_far))
    w_zfar0 = send_two(zfar_send.at[0], zfar_recv.at[0], up)
    put(zfar_send.at[1], z_part(4 + z_far))
    w_zfar1 = send_two(zfar_send.at[1], zfar_recv.at[1], down)
    put(xs_send.at[0], x_part(other * 4 + z_far))
    n_xs0 = send(xs_send.at[0], xs_recv.at[0], x_mate)
    put(znb_send.at[0], z_part(4 + z_up))
    n_znb0 = send(znb_send.at[0], znb_recv.at[0], up)
    put(znb_send.at[1], z_part(z_down))
    n_znb1 = send(znb_send.at[1], znb_recv.at[1], down)
    put(xs_send.at[1], x_part(other * 4 + z_up))
    n_xs1 = send(xs_send.at[1], xs_recv.at[1], x_mate)
    put(z_wait.at[0], z_part(z_up))
    put(z_wait.at[1], z_part(4 + z_down))
    put(xs_send.at[2], x_part(other * 4 + z_down))
    n_xs2 = send(xs_send.at[2], xs_recv.at[2], x_mate)

    w_znb = [], []
    for part in range(2):
        for k, (w_far, to) in enumerate(((w_zfar0, up), (w_zfar1, down))):
            arrived(*w_far[part])
            for i in range(3 * part, 3 * part + 3):
                znb_send[2 + k, i] = (z_wait[k, i] + zfar_recv[k, i].astype(F32)).astype(BF16)
            ref = znb_recv.at[2 + k].at[thirds[part]]
            w_znb[part].append((send(znb_send.at[2 + k].at[thirds[part]], ref, to), ref))
    put(xs_send.at[3], x_part(other * 4 + z))
    n_xs3 = send(xs_send.at[3], xs_recv.at[3], x_mate)
    first, second = pl.ds(0, 2), pl.ds(2, XS - 2)
    arrived(n_xs0, xs_recv.at[0])
    put(xfar_send, x_part(lo * 4 + z_far), (xs_recv.at[0], 0))
    n_xfar0 = send(xfar_send.at[first], xfar_recv.at[first], up)
    n_xfar1 = send(xfar_send.at[second], xfar_recv.at[second], down)
    for n, ref in full_waits:
        arrived(n, ref)
    n_call = send(call.at[core], call.at[core], sibling)
    put(z_mine.at[1], z_part(other * 4 + z))
    put(z_mine.at[0], z_part(lo * 4 + z))
    put(x_mine, x_part(lo * 4 + z))
    arrived(n_xs1, xs_recv.at[1])
    arrived(n_xfar0, xfar_recv.at[first])
    put(xnb_send.at[0], x_part(lo * 4 + z_up), (xs_recv.at[1], 0), (xfar_recv.at[first], 0))
    n_xnb0 = send(xnb_send.at[0], xnb_recv.at[0], up)
    arrived(n_xs2, xs_recv.at[2])
    arrived(n_xfar1, xfar_recv.at[second])
    put(xnb_send.at[1], x_part(lo * 4 + z_down), (xs_recv.at[2], 0), (xfar_recv.at[second], 2))
    n_xnb1 = send(xnb_send.at[1], xnb_recv.at[1], down)

    arrived(n_znb0, znb_recv.at[0])
    arrived(n_znb1, znb_recv.at[1])

    def z_sum(k, which, i):
        return (z_mine[k, i] + znb_recv[2 - 2 * which, i].astype(F32)
                + znb_recv[1 + 2 * which, i].astype(F32))

    w_zx = []
    for part in range(2):
        for wait in w_znb[part]:
            arrived(*wait)
        for i in range(3 * part, 3 * part + 3):
            zx_send[i] = z_sum(1, other, i).astype(BF16)
        ref = zx_recv.at[thirds[part]]
        w_zx.append((send(zx_send.at[thirds[part]], ref, x_mate), ref))

    arrived(n_call, call.at[1 - core])
    for half in range(2):
        for q in range(8):
            coeffs[q * 8:(q + 1) * 8, half * HALF:(half + 1) * HALF] = call[half, q]
    row_lane = lax.broadcasted_iota(jnp.int32, (ND, BS), 1)

    def finish(i, value):
        live = row_lane < block_sizes[aux * OWN + i]
        coulomb[i] = jnp.where(live, value, 0.0).astype(BF16)

    for i in range(ZS):
        z_mine[0, i] = z_sum(0, lo, i)
    arrived(n_xs3, xs_recv.at[3])
    arrived(n_xnb0, xnb_recv.at[0])
    arrived(n_xnb1, xnb_recv.at[1])
    for i in range(XS):
        finish(i, x_mine[i] + xs_recv[3, i].astype(F32) + xnb_recv[0, i].astype(F32)
               + xnb_recv[1, i].astype(F32))
    for wait in w_zx:
        arrived(*wait)
    for i in range(ZS):
        finish(XS + i, z_mine[0, i] + zx_recv[i].astype(F32))

    for copy in sent:
        copy.wait_send()


NSEMS = 240


def deliver(coulomb, coeffs, coulomb_out, coeffs_out):
    coulomb_out[...] = coulomb[...]
    coeffs_out[...] = coeffs[...]


def shards(slab, density, block_list, block_sizes, metric):
    vmem = pl.BlockSpec(memory_space=pltpu.VMEM)
    smem = pl.BlockSpec(memory_space=pltpu.SMEM)
    hbm = pl.BlockSpec(memory_space=pl.ANY)
    coulomb, coeffs = pl.pallas_call(
        kernel,
        out_shape=(
            jax.ShapeDtypeStruct((OWN, ND, BS), BF16),
            jax.ShapeDtypeStruct((ND, AUX), F32),
        ),
        in_specs=[smem, smem, hbm, hbm, hbm],
        out_specs=(vmem, vmem),
        scratch_shapes=[
            pltpu.VMEM((ROWS, AUX), BF16),
            pltpu.VMEM((2048, 16, BS), BF16),
            pltpu.VMEM((ND, ROWS), BF16),
            pltpu.VMEM((2, ND, 256), F32),
            pltpu.VMEM((2, 2, ND, 256), F32),
            pltpu.VMEM((8, 8, HALF), F32),
            pltpu.VMEM((7, 8, HALF), F32),
            pltpu.VMEM((1280, 3 * HB), F32),
            pltpu.VMEM((5, 512, 256), BF16),
            pltpu.VMEM((5, 512, 256), BF16),
            pltpu.VMEM((8, 3 * HALF), F32),
            pltpu.VMEM((8, 3 * HALF), F32),
            pltpu.VMEM((16, 3 * HALF), F32),
            pltpu.VMEM((8, HALF), F32),
            pltpu.VMEM((2, 8, HALF), F32),
            pltpu.VMEM((2, 8, 8, HALF), F32),
            pltpu.VMEM((2, 8, 16, 256), BF16),
            pltpu.VMEM((ND, AUX), BF16),
            pltpu.VMEM((2, ZS, ND, BS), F32),
            pltpu.VMEM((2, ZS, ND, BS), BF16),
            pltpu.VMEM((2, ZS, ND, BS), BF16),
            pltpu.VMEM((4, ZS, ND, BS), BF16),
            pltpu.VMEM((4, ZS, ND, BS), BF16),
            pltpu.VMEM((ZS, ND, BS), BF16),
            pltpu.VMEM((ZS, ND, BS), BF16),
            pltpu.VMEM((2, ZS, ND, BS), F32),
            pltpu.VMEM((4, XS, ND, BS), BF16),
            pltpu.VMEM((4, XS, ND, BS), BF16),
            pltpu.VMEM((XS, ND, BS), BF16),
            pltpu.VMEM((XS, ND, BS), BF16),
            pltpu.VMEM((2, XS, ND, BS), BF16),
            pltpu.VMEM((2, XS, ND, BS), BF16),
            pltpu.VMEM((XS, ND, BS), F32),
            pltpu.SMEM((4 * SLOTS,), jnp.int32),
            pltpu.SemaphoreType.DMA((NCHUNK,)),
            pltpu.SemaphoreType.DMA((4,)),
            pltpu.SemaphoreType.DMA((NSEMS,)),
            pltpu.SemaphoreType.DMA((NSEMS,)),
        ],
        compiler_params=pltpu.CompilerParams(
            collective_id=0, has_side_effects=True, vmem_limit_bytes=56 * 1024 * 1024
        ),
        cost_estimate=pl.CostEstimate(flops=4 * ND * ROWS * AUX, bytes_accessed=2 * ROWS * AUX, transcendentals=0),
    )(block_list, block_sizes, density.reshape(16, 16, BS), slab, metric)
    return pl.pallas_call(
        deliver,
        out_shape=(
            jax.ShapeDtypeStruct(coulomb.shape, coulomb.dtype),
            jax.ShapeDtypeStruct(coeffs.shape, coeffs.dtype),
        ),
        in_specs=[vmem, vmem],
        out_specs=(vmem, vmem),
    )(coulomb, coeffs)


def solution(mesh):
    return jax.shard_map(
        shards,
        mesh=mesh,
        in_specs=(
            P("pair", "aux"),
            P(("pair", "aux"), None, None),
            P("pair"),
            P("pair"),
            P("aux", None),
        ),
        out_specs=(P(("pair", "aux"), None, None), P(None, "aux")),
        check_vma=False,
    )
```

```python
import jax
import jax.numpy as jnp
from jax import lax
from jax.experimental import pallas as pl
from jax.experimental.pallas import tpu as pltpu
from jax.sharding import PartitionSpec as P

F32 = jnp.float32
BF16 = jnp.bfloat16
BS = 128
HB = 128
ND = 64
SLOTS = 88
OWN = 11
AUX = 1024
HALF = 512
ROWS = SLOTS * BS
XS = 5
ZS = OWN - XS
CHUNK = 1024
NCHUNK = ROWS // CHUNK

PARTS = (
    (0, 5, 0, (0, 1, 2)),
    (5, 5, 640, (1, 2, 0)),
    (10, 6, 1280, (2, 0, 1)),
)


def mod(value, size):
    return lax.rem(value + size, size)


def kernel(block_list, block_sizes, density, slab, metric, coulomb, coeffs, *scratch):
    (slab_v, held, picked, acc, sib_acc, fit_send, fit_recv, mw, wh, wl, u0, u, lh,
     own_u, halo, call, rounded, cb, z_wait, x_wait, zfar_send, zfar_recv, znb_send, znb_recv, zx_send, zx_recv, z_mine,
     xs_send, xs_recv, xfar_send, xfar_recv, xnb_send, xnb_recv, x_mine, index, slab_sem, local_sem, send_sem, recv_sem) = scratch

    pair = lax.axis_index("pair")
    aux = lax.axis_index("aux")
    core = lax.rem(pair, 2)
    chip = pair // 2
    x = (chip // 4) * 2 + aux // 4
    y = lax.rem(chip, 4)
    z = lax.rem(aux, 4)

    def device(coords, at_core):
        ax, ay, az = coords
        return (((ax // 2) * 4 + ay) * 2 + at_core, lax.rem(ax, 2) * 4 + az)

    moves = {}
    for dim in range(3):
        for by in (1, -1, 2):
            coords = [x, y, z]
            coords[dim] = mod(coords[dim] + by, 4)
            moves[dim, by] = device(coords, core)

    def moved(dim, by):
        return moves[dim, by]

    sibling = device([x, y, z], 1 - core)
    ext_aux = mod(aux + 2 * core - 1, 8)
    ext = (chip * 2 + (1 - core), ext_aux)
    steps = ((1, 2), (1, 1), (1, 3), (1, 0), (0, 2), (0, 1), (0, 3))
    chip_to = [mod(chip // 4 + flip, 2) * 4 + mod(y + by, 4) for flip, by in steps]
    chip_from = [mod(chip // 4 + flip, 2) * 4 + mod(y - by, 4) for flip, by in steps]
    chips = [(to * 2 + core, aux) for to in chip_to]
    other_cores = [(to * 2 + 1 - core, aux) for to in chip_to]
    x_mate = (pair, mod(aux + 4, 8))

    barrier = pltpu.get_barrier_semaphore()
    partners = chips + other_cores
    partners += [ext, moves[2, 2], moves[0, 1], moves[0, -1], moves[2, 1], moves[2, -1], sibling]
    for partner in partners:
        pl.semaphore_signal(barrier, inc=1, device_id=partner, device_id_type=pl.DeviceIdType.MESH)

    slab_copies = []
    for n in range(NCHUNK):
        rows = pl.ds(n * CHUNK, CHUNK)
        slab_copies.append(pltpu.make_async_copy(slab.at[rows, :], slab_v.at[rows, :], slab_sem.at[n]))

    own_metric = pltpu.make_async_copy(
        metric.at[pl.ds(pl.multiple_of(core * 128, 128), 896), :],
        mw.at[pl.ds(pl.multiple_of(384 - core * 384, 128), 896), :],
        local_sem.at[0],
    )
    own_metric.start()

    def place(part, far3=0, far2=0, far1=0):
        _, tiles, base, _ = PARTS[part]
        return base + core * (64 * tiles) + ((far3 * 4 + far2) * 4 + far1) * tiles

    own_tiles = []
    for part, (first, tiles, _, _) in enumerate(PARTS):
        copy = pltpu.make_async_copy(
            density.at[pl.ds(first, tiles)],
            held.at[pl.ds(place(part), tiles)],
            local_sem.at[1 + part],
        )
        copy.start()
        own_tiles.append(copy)

    pl.semaphore_wait(barrier, len(partners))
    for copy in own_tiles:
        copy.wait()

    count = [0]
    sent = []

    def send(src, dst, to):
        n = count[0]
        count[0] += 1
        copy = pltpu.make_async_remote_copy(
            src_ref=src, dst_ref=dst, send_sem=send_sem.at[n], recv_sem=recv_sem.at[n],
            device_id=to, device_id_type=pl.DeviceIdType.MESH,
        )
        copy.start()
        sent.append(copy)
        return n

    def arrived(n, ref):
        pltpu.make_async_remote_copy(
            src_ref=ref, dst_ref=ref, send_sem=send_sem.at[n], recv_sem=recv_sem.at[n],
            device_id=sibling, device_id_type=pl.DeviceIdType.MESH,
        ).wait_recv()

    def window(start, size):
        return held.at[pl.ds(start, size)]

    sib_waits = []

    def to_sibling(part, start, size):
        _, tiles, _, _ = PARTS[part]
        ref = window(start, size)
        n = send(ref, ref, sibling)
        other = start + (1 - 2 * core) * 64 * tiles
        sib_waits.append((n, window(other, size)))

    class Ring:
        def __init__(self, part, level, first, tiles, cut=0):
            self.part, self.first, self.size = part, first, tiles
            self.cut = cut
            self.dim = PARTS[part][3][level]
            self.stride = PARTS[part][1] * 4 ** level

        def piece(self, far, start=0, size=None):
            return window(self.first + far * self.stride + start, self.size if size is None else size)

        def start(self):
            self.up = send(self.piece(0), self.piece(3), moved(self.dim, 1))
            self.down = send(self.piece(0), self.piece(1), moved(self.dim, -1))
            if self.cut == 0:
                self.far = send(self.piece(0), self.piece(2), moved(self.dim, 2))

        def middle(self):
            arrived(self.up, self.piece(3))
            if self.cut:
                self.up_far = send(self.piece(3, 0, self.cut), self.piece(2, 0, self.cut), moved(self.dim, 1))
            arrived(self.down, self.piece(1))
            if self.cut:
                rest = self.size - self.cut
                self.down_far = send(self.piece(1, self.cut, rest), self.piece(2, self.cut, rest),
                                     moved(self.dim, -1))

        def end(self):
            if self.cut == 0:
                arrived(self.far, self.piece(2))
                return
            arrived(self.up_far, self.piece(2, 0, self.cut))
            arrived(self.down_far, self.piece(2, self.cut, self.size - self.cut))

    def every(make):
        return [make(part, PARTS[part][1]) for part in range(3)]

    first_rings = every(lambda part, t: Ring(part, 0, place(part), t))
    second_own = every(lambda part, t: Ring(part, 1, place(part), t))
    second_rest = every(lambda part, t: Ring(part, 1, place(part) + t, 3 * t))
    third_own = every(lambda part, t: Ring(part, 2, place(part), t, t // 2))
    third_rest = every(lambda part, t: Ring(part, 2, place(part) + t, 3 * t, 3 * t // 2))
    third_rows = [None] + [
        every(lambda part, t, far=far: Ring(part, 2, place(part, 0, far), 4 * t, 2 * t)) for far in (1, 2, 3)
    ]

    def share(far3, far2, rows=1):
        for part in range(3):
            to_sibling(part, place(part, far3, far2), 4 * rows * PARTS[part][1])

    for ring in first_rings + second_own + third_own:
        ring.start()
    for copy in slab_copies:
        copy.start()

    def send_metric(start, rows):
        src = pl.multiple_of(core * 640 + start, 128)
        dst = pl.multiple_of(896 - core * 896 + start, 128)
        here = pl.multiple_of(core * 896 + start, 128)
        n = send(metric.at[pl.ds(src, rows), :], mw.at[pl.ds(dst, rows), :], ext)
        return n, mw.at[pl.ds(here, rows), :]

    metric_waits = [send_metric(0, 128)]

    def find(s, _):
        b = block_list[s]
        j = b & 3
        bz = (b >> 2) & 3
        blo = (b >> 4) & 1
        bc = (b >> 5) & 1
        by = (b >> 6) & 3
        bx = ((b >> 8) & 1) * 2 + blo
        bx, by, bz = (bx - x) & 3, (by - y) & 3, (bz - z) & 3
        places = (
            (((bc * 4 + bz) * 4 + by) * 4 + bx) * 5,
            640 + (((bc * 4 + bx) * 4 + bz) * 4 + by) * 5 - 5,
            1280 + (((bc * 4 + by) * 4 + bx) * 4 + bz) * 6 - 10,
        )
        for r in range(4):
            t = j * 4 + r
            index[s * 4 + r] = t + jnp.where(t < 5, places[0], jnp.where(t < 10, places[1], places[2]))
        return 0

    lax.fori_loop(0, SLOTS // 2, find, 0)
    for ring in first_rings:
        ring.middle()
    for ring in first_rings:
        ring.end()
    for ring in second_rest + third_rest:
        ring.start()
    share(0, 0)
    for ring in third_own + second_own:
        ring.middle()
    lax.fori_loop(SLOTS // 2, SLOTS, find, 0)
    for ring in second_rest:
        ring.middle()
    for ring in third_rows[3] + third_rows[1]:
        ring.start()
    share(0, 3)
    share(0, 1)
    for ring in second_own + second_rest:
        ring.end()
    for ring in third_rows[2]:
        ring.start()
    share(0, 2)
    eye = (lax.broadcasted_iota(jnp.int32, (HB, HB), 0) == lax.broadcasted_iota(jnp.int32, (HB, HB), 1))
    low_ok = jnp.logical_or(aux > 0, core == 1)
    high_ok = jnp.logical_or(aux < 7, core == 0)
    zero_block = jnp.zeros((HB, HB), BF16)

    def build(i):
        for half in range(2):
            n = 2 * i + half
            rows = pl.ds(pl.multiple_of(n * HB, HB), HB)
            middle = mw[rows, HB:2 * HB]
            diag = jnp.sum(jnp.where(eye, middle, 0.0), axis=1, keepdims=True)
            keep = jnp.logical_and(jnp.logical_or(n > 2, low_ok), jnp.logical_or(n < 7, high_ok))
            scale = jnp.where(keep, -1.0 / diag, 0.0)
            for k in range(3):
                block = mw[rows, k * HB:(k + 1) * HB]
                if k == 1:
                    block = jnp.where(eye, 0.0, block)
                block = (block * scale).T
                high = block.astype(BF16)
                low = (block - high.astype(F32)).astype(BF16)
                at = (k + half) * HB
                wh[i, at:at + HB, half * HB:(half + 1) * HB] = high
                wl[i, at:at + HB, half * HB:(half + 1) * HB] = low
            at = (3 - 3 * half) * HB
            wh[i, at:at + HB, half * HB:(half + 1) * HB] = zero_block
            wl[i, at:at + HB, half * HB:(half + 1) * HB] = zero_block
        return 0


    for ring in third_rest:
        ring.middle()
    share(3, 0)
    share(1, 0)
    for far in (3, 1, 2):
        for ring in third_rows[far]:
            ring.middle()
        share(3, far)
        share(1, far)
    metric_waits.append(send_metric(128, 256))
    own_metric.wait()
    lax.fori_loop(0, 3, lambda i, _: build(2 - 2 * core + i), 0)
    diag_rows = []
    for n in range(3, 7):
        middle = mw[n * HB:(n + 1) * HB, HB:2 * HB]
        diag_rows.append(jnp.sum(jnp.where(eye, middle, 0.0), axis=0, keepdims=True))
    diag_row = jnp.concatenate(diag_rows, axis=1)
    for ring in third_own + third_rest:
        ring.end()
    share(2, 0)
    for far in (3, 1, 2):
        for ring in third_rows[far]:
            ring.end()
        share(2, far)
    for n, ref in sib_waits:
        arrived(n, ref)

    lane = lax.broadcasted_iota(jnp.int32, (16, BS), 1)

    def pick(s, _):
        live = jnp.where(lane < block_sizes[s], 1.0, 0.0).astype(BF16)
        column = pl.ds(pl.multiple_of(s * BS, BS), BS)
        for r in range(4):
            picked[r * 16:(r + 1) * 16, column] = held[index[s * 4 + r]] * live
        return 0

    lax.fori_loop(0, SLOTS, pick, 0, unroll=8)

    for copy in slab_copies:
        copy.wait()

    def fit(out, half):
        def step(n, _):
            columns = pl.ds(pl.multiple_of(half * HALF + n * 256, 256), 256)
            out[n] = jnp.dot(picked[...], slab_v[:, columns], preferred_element_type=F32)
            return 0

        for n in range(2):
            step(n, 0)

    fit(sib_acc.at[0], 1 - core)
    n = send(sib_acc.at[0], sib_acc.at[1], sibling)
    fit(acc, core)
    arrived(n, sib_acc.at[1])
    for q in range(8):
        for n in range(2):
            rows = slice(q * 8, (q + 1) * 8)
            fit_send[q, :, n * 256:(n + 1) * 256] = acc[n, rows, :] + sib_acc[1, n, rows, :]
    waits = []
    for o, to in enumerate(chip_to):
        n = send(fit_send.at[to], fit_recv.at[o], chips[o])
        waits.append((n, fit_recv.at[o]))
    for n, ref in metric_waits:
        arrived(n, ref)
    lax.fori_loop(0, 2, lambda i, _: build(3 * core + i), 0)
    total = fit_send[chip]
    for o, (n, ref) in enumerate(waits):
        arrived(n, ref)
        total = total + fit_recv[o]

    own_u[...] = total / diag_row
    n_sib = send(own_u, halo.at[core], sibling)
    n_ext = send(own_u, halo.at[1 - core], ext)
    u0[:, HALF:2 * HALF] = own_u[...]
    arrived(n_sib, halo.at[1 - core])
    arrived(n_ext, halo.at[core])
    u0[:, :HALF] = jnp.where(low_ok, halo[0], 0.0)
    u0[:, 2 * HALF:] = jnp.where(high_ok, halo[1], 0.0)
    u[...] = u0[...]
    for pairs in ((0, 1, 2, 3, 4), (0, 1, 2, 3, 4), (1, 2, 3), (1, 2, 3)):
        values = u[...]
        high = values.astype(BF16)
        lh[0:8, :] = values
        lh[8:16, :] = values - high.astype(F32)
        for i in pairs:
            left = lh[:, i * 256:i * 256 + 512].astype(BF16)
            one = jnp.dot(left, wh[i], preferred_element_type=F32)
            two = jnp.dot(left, wl[i], preferred_element_type=F32)
            cols = slice((2 * i + 1) * HB, (2 * i + 3) * HB)
            u[:, cols] = u0[:, cols] + (one[0:8] + (one[8:16] + two[0:8]))

    own = u[:, HALF:2 * HALF]
    call[core, chip] = own
    rounded[core, chip] = jnp.concatenate([own[:, :256], own[:, 256:]], axis=0).astype(BF16)
    ref = rounded.at[core, chip]
    waits = []
    for o, source in enumerate(chip_from):
        waits.append((send(ref, ref, chips[o]), rounded.at[core, source]))
        waits.append((send(ref, ref, other_cores[o]), rounded.at[1 - core, source]))
    waits.append((send(ref, ref, sibling), rounded.at[1 - core, chip]))
    ref = call.at[core, chip]
    full_waits = [(send(ref, ref, chips[o]), call.at[core, source]) for o, source in enumerate(chip_from)]
    for n, ref in waits:
        arrived(n, ref)
    for half in range(2):
        for q in range(4):
            two = [rounded[half, 2 * q + k].astype(F32) for k in range(2)]
            for k in range(2):
                part = slice(k * 8, (k + 1) * 8)
                cb[q * 16:(q + 1) * 16, half * HALF + k * 256:half * HALF + (k + 1) * 256] = (
                    jnp.concatenate([two[0][part], two[1][part]], axis=0).astype(BF16))

    def dots(to, start, slots):
        rows = pl.ds(pl.multiple_of(to * (OWN * BS) + start * BS, BS), slots * BS)
        return lax.dot_general(cb[...], slab_v[rows, :], (((1,), (1,)), ((), ())),
                               preferred_element_type=F32)

    def put(ref, value, *terms):
        slots = value.shape[1] // BS
        for k in range(slots):
            part = value[:, k * BS:(k + 1) * BS]
            for term, first in terms:
                if first <= k < first + term.shape[0]:
                    part = part + term[k - first].astype(F32)
            ref[k] = part.astype(ref.dtype)

    def z_part(to):
        return dots(to, XS, ZS)

    def x_part(to):
        return dots(to, 0, XS)

    up, down = moved(2, 1), moved(2, -1)
    z_up, z_down, z_far = mod(z + 1, 4), mod(z - 1, 4), mod(z + 2, 4)
    lo = aux // 4
    other = 1 - lo

    thirds = (pl.ds(0, 3), pl.ds(3, ZS - 3))

    def send_two(src, dst, to):
        return [(send(src.at[part], dst.at[part], to), dst.at[part]) for part in thirds]

    def x_out(k, to):
        put(xs_send.at[k], x_part(other * 4 + to))
        return send(xs_send.at[k], xs_recv.at[k], x_mate)

    n_xs0 = x_out(0, z_far)
    put(zfar_send.at[0], z_part(z_far))
    w_zfar0 = send_two(zfar_send.at[0], zfar_recv.at[0], up)
    put(zfar_send.at[1], z_part(4 + z_far))
    w_zfar1 = send_two(zfar_send.at[1], zfar_recv.at[1], down)
    n_xs1 = x_out(1, z_up)
    n_xs2 = x_out(2, z_down)
    put(znb_send.at[0], z_part(4 + z_up))
    n_znb0 = send(znb_send.at[0], znb_recv.at[0], up)
    put(znb_send.at[1], z_part(z_down))
    n_znb1 = send(znb_send.at[1], znb_recv.at[1], down)
    put(z_wait.at[0], z_part(z_up))
    put(z_wait.at[1], z_part(4 + z_down))

    w_znb = [], []

    def pass_on(part):
        for k, (w_far, to) in enumerate(((w_zfar0, up), (w_zfar1, down))):
            arrived(*w_far[part])
            for i in range(3 * part, 3 * part + 3):
                znb_send[2 + k, i] = (z_wait[k, i] + zfar_recv[k, i].astype(F32)).astype(BF16)
            ref = znb_recv.at[2 + k].at[thirds[part]]
            w_znb[part].append((send(znb_send.at[2 + k].at[thirds[part]], ref, to), ref))

    pass_on(0)
    first, second = pl.ds(0, 2), pl.ds(2, XS - 2)
    put(x_mine, x_part(lo * 4 + z_far))
    arrived(n_xs0, xs_recv.at[0])
    for i in range(XS):
        xfar_send[i] = (x_mine[i] + xs_recv[0, i].astype(F32)).astype(BF16)
    n_xfar0 = send(xfar_send.at[first], xfar_recv.at[first], up)
    n_xfar1 = send(xfar_send.at[second], xfar_recv.at[second], down)
    pass_on(1)
    n_xs3 = x_out(3, z)
    put(x_wait.at[0], x_part(lo * 4 + z_up))
    put(x_wait.at[1], x_part(lo * 4 + z_down))
    for n, ref in full_waits:
        arrived(n, ref)
    n_call = send(call.at[core], call.at[core], sibling)
    put(z_mine.at[1], z_part(other * 4 + z))
    put(z_mine.at[0], z_part(lo * 4 + z))
    arrived(n_xs1, xs_recv.at[1])
    arrived(n_xfar0, xfar_recv.at[first])
    for i in range(XS):
        value = x_wait[0, i] + xs_recv[1, i].astype(F32)
        xnb_send[0, i] = ((value + xfar_recv[i].astype(F32)) if i < 2 else value).astype(BF16)
    n_xnb0 = send(xnb_send.at[0], xnb_recv.at[0], up)
    arrived(n_xs2, xs_recv.at[2])
    arrived(n_xfar1, xfar_recv.at[second])
    for i in range(XS):
        value = x_wait[1, i] + xs_recv[2, i].astype(F32)
        xnb_send[1, i] = ((value + xfar_recv[i].astype(F32)) if i >= 2 else value).astype(BF16)
    n_xnb1 = send(xnb_send.at[1], xnb_recv.at[1], down)

    arrived(n_znb0, znb_recv.at[0])
    arrived(n_znb1, znb_recv.at[1])

    def z_sum(k, which, i):
        return (z_mine[k, i] + znb_recv[2 - 2 * which, i].astype(F32)
                + znb_recv[1 + 2 * which, i].astype(F32))

    put(x_mine, x_part(lo * 4 + z))
    w_zx = []
    for part in range(2):
        for wait in w_znb[part]:
            arrived(*wait)
        for i in range(3 * part, 3 * part + 3):
            zx_send[i] = z_sum(1, other, i).astype(BF16)
        ref = zx_recv.at[thirds[part]]
        w_zx.append((send(zx_send.at[thirds[part]], ref, x_mate), ref))

    arrived(n_call, call.at[1 - core])
    for half in range(2):
        for q in range(8):
            coeffs[q * 8:(q + 1) * 8, half * HALF:(half + 1) * HALF] = call[half, q]
    row_lane = lax.broadcasted_iota(jnp.int32, (ND, BS), 1)

    def finish(i, value):
        live = row_lane < block_sizes[aux * OWN + i]
        coulomb[i] = jnp.where(live, value, 0.0).astype(BF16)

    for i in range(ZS):
        z_mine[0, i] = z_sum(0, lo, i)
    arrived(n_xs3, xs_recv.at[3])
    arrived(n_xnb0, xnb_recv.at[0])
    arrived(n_xnb1, xnb_recv.at[1])
    for i in range(XS):
        finish(i, x_mine[i] + xs_recv[3, i].astype(F32) + xnb_recv[0, i].astype(F32)
               + xnb_recv[1, i].astype(F32))
    for wait in w_zx:
        arrived(*wait)
    for i in range(ZS):
        finish(XS + i, z_mine[0, i] + zx_recv[i].astype(F32))

    for copy in sent:
        copy.wait_send()


NSEMS = 240


def deliver(coulomb, coeffs, coulomb_out, coeffs_out):
    coulomb_out[...] = coulomb[...]
    coeffs_out[...] = coeffs[...]


def shards(slab, density, block_list, block_sizes, metric):
    vmem = pl.BlockSpec(memory_space=pltpu.VMEM)
    smem = pl.BlockSpec(memory_space=pltpu.SMEM)
    hbm = pl.BlockSpec(memory_space=pl.ANY)
    coulomb, coeffs = pl.pallas_call(
        kernel,
        out_shape=(
            jax.ShapeDtypeStruct((OWN, ND, BS), BF16),
            jax.ShapeDtypeStruct((ND, AUX), F32),
        ),
        in_specs=[smem, smem, hbm, hbm, hbm],
        out_specs=(vmem, vmem),
        scratch_shapes=[
            pltpu.VMEM((ROWS, AUX), BF16),
            pltpu.VMEM((2048, 16, BS), BF16),
            pltpu.VMEM((ND, ROWS), BF16),
            pltpu.VMEM((2, ND, 256), F32),
            pltpu.VMEM((2, 2, ND, 256), F32),
            pltpu.VMEM((8, 8, HALF), F32),
            pltpu.VMEM((7, 8, HALF), F32),
            pltpu.VMEM((1280, 3 * HB), F32),
            pltpu.VMEM((5, 512, 256), BF16),
            pltpu.VMEM((5, 512, 256), BF16),
            pltpu.VMEM((8, 3 * HALF), F32),
            pltpu.VMEM((8, 3 * HALF), F32),
            pltpu.VMEM((16, 3 * HALF), F32),
            pltpu.VMEM((8, HALF), F32),
            pltpu.VMEM((2, 8, HALF), F32),
            pltpu.VMEM((2, 8, 8, HALF), F32),
            pltpu.VMEM((2, 8, 16, 256), BF16),
            pltpu.VMEM((ND, AUX), BF16),
            pltpu.VMEM((2, ZS, ND, BS), F32),
            pltpu.VMEM((2, XS, ND, BS), F32),
            pltpu.VMEM((2, ZS, ND, BS), BF16),
            pltpu.VMEM((2, ZS, ND, BS), BF16),
            pltpu.VMEM((4, ZS, ND, BS), BF16),
            pltpu.VMEM((4, ZS, ND, BS), BF16),
            pltpu.VMEM((ZS, ND, BS), BF16),
            pltpu.VMEM((ZS, ND, BS), BF16),
            pltpu.VMEM((2, ZS, ND, BS), F32),
            pltpu.VMEM((4, XS, ND, BS), BF16),
            pltpu.VMEM((4, XS, ND, BS), BF16),
            pltpu.VMEM((XS, ND, BS), BF16),
            pltpu.VMEM((XS, ND, BS), BF16),
            pltpu.VMEM((2, XS, ND, BS), BF16),
            pltpu.VMEM((2, XS, ND, BS), BF16),
            pltpu.VMEM((XS, ND, BS), F32),
            pltpu.SMEM((4 * SLOTS,), jnp.int32),
            pltpu.SemaphoreType.DMA((NCHUNK,)),
            pltpu.SemaphoreType.DMA((4,)),
            pltpu.SemaphoreType.DMA((NSEMS,)),
            pltpu.SemaphoreType.DMA((NSEMS,)),
        ],
        compiler_params=pltpu.CompilerParams(
            collective_id=0, has_side_effects=True, vmem_limit_bytes=56 * 1024 * 1024
        ),
        cost_estimate=pl.CostEstimate(flops=4 * ND * ROWS * AUX, bytes_accessed=2 * ROWS * AUX, transcendentals=0),
    )(block_list, block_sizes, density.reshape(16, 16, BS), slab, metric)
    return pl.pallas_call(
        deliver,
        out_shape=(
            jax.ShapeDtypeStruct(coulomb.shape, coulomb.dtype),
            jax.ShapeDtypeStruct(coeffs.shape, coeffs.dtype),
        ),
        in_specs=[vmem, vmem],
        out_specs=(vmem, vmem),
    )(coulomb, coeffs)


def solution(mesh):
    return jax.shard_map(
        shards,
        mesh=mesh,
        in_specs=(
            P("pair", "aux"),
            P(("pair", "aux"), None, None),
            P("pair"),
            P("pair"),
            P("aux", None),
        ),
        out_specs=(P(("pair", "aux"), None, None), P(None, "aux")),
        check_vma=False,
    )
```

```python
import jax
import jax.numpy as jnp
from jax import lax
from jax.experimental import pallas as pl
from jax.experimental.pallas import tpu as pltpu
from jax.sharding import PartitionSpec as P

F32 = jnp.float32
BF16 = jnp.bfloat16
BS = 128
HB = 128
ND = 64
SLOTS = 88
OWN = 11
AUX = 1024
HALF = 512
ROWS = SLOTS * BS
XS = 5
ZS = OWN - XS
CHUNK = 1024
NCHUNK = ROWS // CHUNK

PARTS = (
    (0, 5, 0, (0, 1, 2)),
    (5, 5, 640, (1, 2, 0)),
    (10, 6, 1280, (2, 0, 1)),
)


def mod(value, size):
    return lax.rem(value + size, size)


def kernel(block_list, block_sizes, density, slab, metric, coulomb, coeffs, *scratch):
    (slab_v, held, picked, acc, sib_acc, fit_send, fit_recv, mw, wh, wl, u0, u, lh,
     own_u, halo, call, rounded, cb, z_wait, x_wait, zfar_send, zfar_recv, znb_send, znb_recv, zx_send, zx_recv, z_mine,
     xs_send, xs_recv, xfar_send, xfar_recv, xnb_send, xnb_recv, x_mine, index, slab_sem, local_sem, send_sem, recv_sem) = scratch

    pair = lax.axis_index("pair")
    aux = lax.axis_index("aux")
    core = lax.rem(pair, 2)
    chip = pair // 2
    x = (chip // 4) * 2 + aux // 4
    y = lax.rem(chip, 4)
    z = lax.rem(aux, 4)

    def device(coords, at_core):
        ax, ay, az = coords
        return (((ax // 2) * 4 + ay) * 2 + at_core, lax.rem(ax, 2) * 4 + az)

    moves = {}
    for dim in range(3):
        for by in (1, -1, 2):
            coords = [x, y, z]
            coords[dim] = mod(coords[dim] + by, 4)
            moves[dim, by] = device(coords, core)

    def moved(dim, by):
        return moves[dim, by]

    sibling = device([x, y, z], 1 - core)
    ext_aux = mod(aux + 2 * core - 1, 8)
    ext = (chip * 2 + (1 - core), ext_aux)
    steps = ((1, 2), (1, 1), (1, 3), (1, 0), (0, 2), (0, 1), (0, 3))
    chip_to = [mod(chip // 4 + flip, 2) * 4 + mod(y + by, 4) for flip, by in steps]
    chip_from = [mod(chip // 4 + flip, 2) * 4 + mod(y - by, 4) for flip, by in steps]
    chips = [(to * 2 + core, aux) for to in chip_to]
    other_cores = [(to * 2 + 1 - core, aux) for to in chip_to]
    x_mate = (pair, mod(aux + 4, 8))

    barrier = pltpu.get_barrier_semaphore()
    partners = chips + other_cores
    partners += [ext, moves[2, 2], moves[0, 1], moves[0, -1], moves[2, 1], moves[2, -1], sibling]
    for partner in partners:
        pl.semaphore_signal(barrier, inc=1, device_id=partner, device_id_type=pl.DeviceIdType.MESH)

    slab_copies = []
    for n in range(NCHUNK):
        rows = pl.ds(n * CHUNK, CHUNK)
        slab_copies.append(pltpu.make_async_copy(slab.at[rows, :], slab_v.at[rows, :], slab_sem.at[n]))

    own_metric = pltpu.make_async_copy(
        metric.at[pl.ds(pl.multiple_of(core * 128, 128), 896), :],
        mw.at[pl.ds(pl.multiple_of(384 - core * 384, 128), 896), :],
        local_sem.at[0],
    )
    own_metric.start()

    def place(part, far3=0, far2=0, far1=0):
        _, tiles, base, _ = PARTS[part]
        return base + core * (64 * tiles) + ((far3 * 4 + far2) * 4 + far1) * tiles

    own_tiles = []
    for part, (first, tiles, _, _) in enumerate(PARTS):
        copy = pltpu.make_async_copy(
            density.at[pl.ds(first, tiles)],
            held.at[pl.ds(place(part), tiles)],
            local_sem.at[1 + part],
        )
        copy.start()
        own_tiles.append(copy)

    pl.semaphore_wait(barrier, len(partners))
    for copy in own_tiles:
        copy.wait()

    count = [0]
    sent = []

    def send(src, dst, to):
        n = count[0]
        count[0] += 1
        copy = pltpu.make_async_remote_copy(
            src_ref=src, dst_ref=dst, send_sem=send_sem.at[n], recv_sem=recv_sem.at[n],
            device_id=to, device_id_type=pl.DeviceIdType.MESH,
        )
        copy.start()
        sent.append(copy)
        return n

    def arrived(n, ref):
        pltpu.make_async_remote_copy(
            src_ref=ref, dst_ref=ref, send_sem=send_sem.at[n], recv_sem=recv_sem.at[n],
            device_id=sibling, device_id_type=pl.DeviceIdType.MESH,
        ).wait_recv()

    def window(start, size):
        return held.at[pl.ds(start, size)]

    sib_waits = []

    def to_sibling(part, start, size):
        _, tiles, _, _ = PARTS[part]
        ref = window(start, size)
        n = send(ref, ref, sibling)
        other = start + (1 - 2 * core) * 64 * tiles
        sib_waits.append((n, window(other, size)))

    class Ring:
        def __init__(self, part, level, first, tiles, cut=0):
            self.part, self.first, self.size = part, first, tiles
            self.cut = cut
            self.dim = PARTS[part][3][level]
            self.stride = PARTS[part][1] * 4 ** level

        def piece(self, far, start=0, size=None):
            return window(self.first + far * self.stride + start, self.size if size is None else size)

        def start(self):
            self.up = send(self.piece(0), self.piece(3), moved(self.dim, 1))
            self.down = send(self.piece(0), self.piece(1), moved(self.dim, -1))
            if self.cut == 0:
                self.far = send(self.piece(0), self.piece(2), moved(self.dim, 2))

        def middle(self):
            arrived(self.up, self.piece(3))
            if self.cut:
                self.up_far = send(self.piece(3, 0, self.cut), self.piece(2, 0, self.cut), moved(self.dim, 1))
            arrived(self.down, self.piece(1))
            if self.cut:
                rest = self.size - self.cut
                self.down_far = send(self.piece(1, self.cut, rest), self.piece(2, self.cut, rest),
                                     moved(self.dim, -1))

        def end(self):
            if self.cut == 0:
                arrived(self.far, self.piece(2))
                return
            arrived(self.up_far, self.piece(2, 0, self.cut))
            arrived(self.down_far, self.piece(2, self.cut, self.size - self.cut))

    def every(make):
        return [make(part, PARTS[part][1]) for part in range(3)]

    first_rings = every(lambda part, t: Ring(part, 0, place(part), t))
    second_own = every(lambda part, t: Ring(part, 1, place(part), t, t // 2))
    second_rest = every(lambda part, t: Ring(part, 1, place(part) + t, 3 * t, 3 * t // 2))
    third_own = every(lambda part, t: Ring(part, 2, place(part), t, t // 2))
    third_rest = every(lambda part, t: Ring(part, 2, place(part) + t, 3 * t, 3 * t // 2))
    third_rows = [None] + [
        every(lambda part, t, far=far: Ring(part, 2, place(part, 0, far), 4 * t, 2 * t)) for far in (1, 2, 3)
    ]

    def share(far3, far2, rows=1):
        for part in range(3):
            to_sibling(part, place(part, far3, far2), 4 * rows * PARTS[part][1])

    for ring in first_rings + second_own + third_own:
        ring.start()
    for copy in slab_copies:
        copy.start()

    def send_metric(start, rows):
        src = pl.multiple_of(core * 640 + start, 128)
        dst = pl.multiple_of(896 - core * 896 + start, 128)
        here = pl.multiple_of(core * 896 + start, 128)
        n = send(metric.at[pl.ds(src, rows), :], mw.at[pl.ds(dst, rows), :], ext)
        return n, mw.at[pl.ds(here, rows), :]

    metric_waits = [send_metric(0, 128)]

    def find(s, _):
        b = block_list[s]
        j = b & 3
        bz = (b >> 2) & 3
        blo = (b >> 4) & 1
        bc = (b >> 5) & 1
        by = (b >> 6) & 3
        bx = ((b >> 8) & 1) * 2 + blo
        bx, by, bz = (bx - x) & 3, (by - y) & 3, (bz - z) & 3
        places = (
            (((bc * 4 + bz) * 4 + by) * 4 + bx) * 5,
            640 + (((bc * 4 + bx) * 4 + bz) * 4 + by) * 5 - 5,
            1280 + (((bc * 4 + by) * 4 + bx) * 4 + bz) * 6 - 10,
        )
        for r in range(4):
            t = j * 4 + r
            index[s * 4 + r] = t + jnp.where(t < 5, places[0], jnp.where(t < 10, places[1], places[2]))
        return 0

    lax.fori_loop(0, SLOTS // 2, find, 0)
    for ring in first_rings:
        ring.middle()
    for ring in first_rings:
        ring.end()
    for ring in second_rest + third_rest:
        ring.start()
    share(0, 0)
    for ring in third_own + second_own:
        ring.middle()
    lax.fori_loop(SLOTS // 2, SLOTS, find, 0)
    for ring in second_rest:
        ring.middle()
    for ring in third_rows[3] + third_rows[1]:
        ring.start()
    share(0, 3)
    share(0, 1)
    for ring in second_own + second_rest:
        ring.end()
    for ring in third_rows[2]:
        ring.start()
    share(0, 2)
    eye = (lax.broadcasted_iota(jnp.int32, (HB, HB), 0) == lax.broadcasted_iota(jnp.int32, (HB, HB), 1))
    low_ok = jnp.logical_or(aux > 0, core == 1)
    high_ok = jnp.logical_or(aux < 7, core == 0)
    zero_block = jnp.zeros((HB, HB), BF16)

    def build(i):
        for half in range(2):
            n = 2 * i + half
            rows = pl.ds(pl.multiple_of(n * HB, HB), HB)
            middle = mw[rows, HB:2 * HB]
            diag = jnp.sum(jnp.where(eye, middle, 0.0), axis=1, keepdims=True)
            keep = jnp.logical_and(jnp.logical_or(n > 2, low_ok), jnp.logical_or(n < 7, high_ok))
            scale = jnp.where(keep, -1.0 / diag, 0.0)
            for k in range(3):
                block = mw[rows, k * HB:(k + 1) * HB]
                if k == 1:
                    block = jnp.where(eye, 0.0, block)
                block = (block * scale).T
                high = block.astype(BF16)
                low = (block - high.astype(F32)).astype(BF16)
                at = (k + half) * HB
                wh[i, at:at + HB, half * HB:(half + 1) * HB] = high
                wl[i, at:at + HB, half * HB:(half + 1) * HB] = low
            at = (3 - 3 * half) * HB
            wh[i, at:at + HB, half * HB:(half + 1) * HB] = zero_block
            wl[i, at:at + HB, half * HB:(half + 1) * HB] = zero_block
        return 0


    for ring in third_rest:
        ring.middle()
    share(3, 0)
    share(1, 0)
    for far in (3, 1, 2):
        for ring in third_rows[far]:
            ring.middle()
        share(3, far)
        share(1, far)
    metric_waits.append(send_metric(128, 256))
    own_metric.wait()
    lax.fori_loop(0, 3, lambda i, _: build(2 - 2 * core + i), 0)
    diag_rows = []
    for n in range(3, 7):
        middle = mw[n * HB:(n + 1) * HB, HB:2 * HB]
        diag_rows.append(jnp.sum(jnp.where(eye, middle, 0.0), axis=0, keepdims=True))
    diag_row = jnp.concatenate(diag_rows, axis=1)
    for ring in third_own + third_rest:
        ring.end()
    share(2, 0)
    for far in (3, 1, 2):
        for ring in third_rows[far]:
            ring.end()
        share(2, far)
    for n, ref in sib_waits:
        arrived(n, ref)

    lane = lax.broadcasted_iota(jnp.int32, (16, BS), 1)

    def pick(s, _):
        live = jnp.where(lane < block_sizes[s], 1.0, 0.0).astype(BF16)
        column = pl.ds(pl.multiple_of(s * BS, BS), BS)
        for r in range(4):
            picked[r * 16:(r + 1) * 16, column] = held[index[s * 4 + r]] * live
        return 0

    lax.fori_loop(0, SLOTS, pick, 0, unroll=8)

    for copy in slab_copies:
        copy.wait()

    def fit(out, half):
        def step(n, _):
            columns = pl.ds(pl.multiple_of(half * HALF + n * 256, 256), 256)
            out[n] = jnp.dot(picked[...], slab_v[:, columns], preferred_element_type=F32)
            return 0

        for n in range(2):
            step(n, 0)

    fit(sib_acc.at[0], 1 - core)
    n = send(sib_acc.at[0], sib_acc.at[1], sibling)
    fit(acc, core)
    arrived(n, sib_acc.at[1])
    for q in range(8):
        for n in range(2):
            rows = slice(q * 8, (q + 1) * 8)
            fit_send[q, :, n * 256:(n + 1) * 256] = acc[n, rows, :] + sib_acc[1, n, rows, :]
    waits = []
    for o, to in enumerate(chip_to):
        n = send(fit_send.at[to], fit_recv.at[o], chips[o])
        waits.append((n, fit_recv.at[o]))
    for n, ref in metric_waits:
        arrived(n, ref)
    lax.fori_loop(0, 2, lambda i, _: build(3 * core + i), 0)
    total = fit_send[chip]
    for o, (n, ref) in enumerate(waits):
        arrived(n, ref)
        total = total + fit_recv[o]

    own_u[...] = total / diag_row
    n_sib = send(own_u, halo.at[core], sibling)
    n_ext = send(own_u, halo.at[1 - core], ext)
    u0[:, HALF:2 * HALF] = own_u[...]
    arrived(n_sib, halo.at[1 - core])
    arrived(n_ext, halo.at[core])
    u0[:, :HALF] = jnp.where(low_ok, halo[0], 0.0)
    u0[:, 2 * HALF:] = jnp.where(high_ok, halo[1], 0.0)
    u[...] = u0[...]
    for pairs in ((0, 1, 2, 3, 4), (0, 1, 2, 3, 4), (1, 2, 3), (1, 2, 3)):
        values = u[...]
        high = values.astype(BF16)
        lh[0:8, :] = values
        lh[8:16, :] = values - high.astype(F32)
        for i in pairs:
            left = lh[:, i * 256:i * 256 + 512].astype(BF16)
            one = jnp.dot(left, wh[i], preferred_element_type=F32)
            two = jnp.dot(left, wl[i], preferred_element_type=F32)
            cols = slice((2 * i + 1) * HB, (2 * i + 3) * HB)
            u[:, cols] = u0[:, cols] + (one[0:8] + (one[8:16] + two[0:8]))

    own = u[:, HALF:2 * HALF]
    call[core, chip] = own
    rounded[core, chip] = jnp.concatenate([own[:, :256], own[:, 256:]], axis=0).astype(BF16)
    ref = rounded.at[core, chip]
    waits = []
    for o, source in enumerate(chip_from):
        waits.append((send(ref, ref, chips[o]), rounded.at[core, source]))
        waits.append((send(ref, ref, other_cores[o]), rounded.at[1 - core, source]))
    waits.append((send(ref, ref, sibling), rounded.at[1 - core, chip]))
    ref = call.at[core, chip]
    full_waits = [(send(ref, ref, chips[o]), call.at[core, source]) for o, source in enumerate(chip_from)]
    for n, ref in waits:
        arrived(n, ref)
    for half in range(2):
        for q in range(4):
            two = [rounded[half, 2 * q + k].astype(F32) for k in range(2)]
            for k in range(2):
                part = slice(k * 8, (k + 1) * 8)
                cb[q * 16:(q + 1) * 16, half * HALF + k * 256:half * HALF + (k + 1) * 256] = (
                    jnp.concatenate([two[0][part], two[1][part]], axis=0).astype(BF16))

    def dots(to, start, slots):
        rows = pl.ds(pl.multiple_of(to * (OWN * BS) + start * BS, BS), slots * BS)
        return lax.dot_general(cb[...], slab_v[rows, :], (((1,), (1,)), ((), ())),
                               preferred_element_type=F32)

    def put(ref, value, *terms):
        slots = value.shape[1] // BS
        for k in range(slots):
            part = value[:, k * BS:(k + 1) * BS]
            for term, first in terms:
                if first <= k < first + term.shape[0]:
                    part = part + term[k - first].astype(F32)
            ref[k] = part.astype(ref.dtype)

    def z_part(to):
        return dots(to, XS, ZS)

    def x_part(to):
        return dots(to, 0, XS)

    up, down = moved(2, 1), moved(2, -1)
    z_up, z_down, z_far = mod(z + 1, 4), mod(z - 1, 4), mod(z + 2, 4)
    lo = aux // 4
    other = 1 - lo

    thirds = (pl.ds(0, 3), pl.ds(3, ZS - 3))

    def send_two(src, dst, to):
        return [(send(src.at[part], dst.at[part], to), dst.at[part]) for part in thirds]

    def x_out(k, to):
        put(xs_send.at[k], x_part(other * 4 + to))
        return send(xs_send.at[k], xs_recv.at[k], x_mate)

    n_xs0 = x_out(0, z_far)
    put(zfar_send.at[0], z_part(z_far))
    w_zfar0 = send_two(zfar_send.at[0], zfar_recv.at[0], up)
    put(zfar_send.at[1], z_part(4 + z_far))
    w_zfar1 = send_two(zfar_send.at[1], zfar_recv.at[1], down)
    n_xs1 = x_out(1, z_up)
    n_xs2 = x_out(2, z_down)
    put(znb_send.at[0], z_part(4 + z_up))
    n_znb0 = send(znb_send.at[0], znb_recv.at[0], up)
    put(znb_send.at[1], z_part(z_down))
    n_znb1 = send(znb_send.at[1], znb_recv.at[1], down)
    put(z_wait.at[0], z_part(z_up))
    put(z_wait.at[1], z_part(4 + z_down))

    w_znb = [], []

    def pass_on(part):
        for k, (w_far, to) in enumerate(((w_zfar0, up), (w_zfar1, down))):
            arrived(*w_far[part])
            for i in range(3 * part, 3 * part + 3):
                znb_send[2 + k, i] = (z_wait[k, i] + zfar_recv[k, i].astype(F32)).astype(BF16)
            ref = znb_recv.at[2 + k].at[thirds[part]]
            w_znb[part].append((send(znb_send.at[2 + k].at[thirds[part]], ref, to), ref))

    pass_on(0)
    first, second = pl.ds(0, 2), pl.ds(2, XS - 2)
    put(x_mine, x_part(lo * 4 + z_far))
    arrived(n_xs0, xs_recv.at[0])
    for i in range(XS):
        xfar_send[i] = (x_mine[i] + xs_recv[0, i].astype(F32)).astype(BF16)
    n_xfar0 = send(xfar_send.at[first], xfar_recv.at[first], up)
    n_xfar1 = send(xfar_send.at[second], xfar_recv.at[second], down)
    pass_on(1)
    n_xs3 = x_out(3, z)
    put(x_wait.at[0], x_part(lo * 4 + z_up))
    put(x_wait.at[1], x_part(lo * 4 + z_down))
    for n, ref in full_waits:
        arrived(n, ref)
    n_call = send(call.at[core], call.at[core], sibling)
    put(z_mine.at[1], z_part(other * 4 + z))
    put(z_mine.at[0], z_part(lo * 4 + z))
    arrived(n_xs1, xs_recv.at[1])
    arrived(n_xfar0, xfar_recv.at[first])
    for i in range(XS):
        value = x_wait[0, i] + xs_recv[1, i].astype(F32)
        xnb_send[0, i] = ((value + xfar_recv[i].astype(F32)) if i < 2 else value).astype(BF16)
    n_xnb0 = send(xnb_send.at[0], xnb_recv.at[0], up)
    arrived(n_xs2, xs_recv.at[2])
    arrived(n_xfar1, xfar_recv.at[second])
    for i in range(XS):
        value = x_wait[1, i] + xs_recv[2, i].astype(F32)
        xnb_send[1, i] = ((value + xfar_recv[i].astype(F32)) if i >= 2 else value).astype(BF16)
    n_xnb1 = send(xnb_send.at[1], xnb_recv.at[1], down)

    arrived(n_znb0, znb_recv.at[0])
    arrived(n_znb1, znb_recv.at[1])

    def z_sum(k, which, i):
        return (z_mine[k, i] + znb_recv[2 - 2 * which, i].astype(F32)
                + znb_recv[1 + 2 * which, i].astype(F32))

    put(x_mine, x_part(lo * 4 + z))
    w_zx = []
    for part in range(2):
        for wait in w_znb[part]:
            arrived(*wait)
        for i in range(3 * part, 3 * part + 3):
            zx_send[i] = z_sum(1, other, i).astype(BF16)
        ref = zx_recv.at[thirds[part]]
        w_zx.append((send(zx_send.at[thirds[part]], ref, x_mate), ref))

    arrived(n_call, call.at[1 - core])
    for half in range(2):
        for q in range(8):
            coeffs[q * 8:(q + 1) * 8, half * HALF:(half + 1) * HALF] = call[half, q]
    row_lane = lax.broadcasted_iota(jnp.int32, (ND, BS), 1)

    def finish(i, value):
        live = row_lane < block_sizes[aux * OWN + i]
        coulomb[i] = jnp.where(live, value, 0.0).astype(BF16)

    for i in range(ZS):
        z_mine[0, i] = z_sum(0, lo, i)
    arrived(n_xs3, xs_recv.at[3])
    arrived(n_xnb0, xnb_recv.at[0])
    arrived(n_xnb1, xnb_recv.at[1])
    for i in range(XS):
        finish(i, x_mine[i] + xs_recv[3, i].astype(F32) + xnb_recv[0, i].astype(F32)
               + xnb_recv[1, i].astype(F32))
    for wait in w_zx:
        arrived(*wait)
    for i in range(ZS):
        finish(XS + i, z_mine[0, i] + zx_recv[i].astype(F32))

    for copy in sent:
        copy.wait_send()


NSEMS = 240


def deliver(coulomb, coeffs, coulomb_out, coeffs_out):
    coulomb_out[...] = coulomb[...]
    coeffs_out[...] = coeffs[...]


def shards(slab, density, block_list, block_sizes, metric):
    vmem = pl.BlockSpec(memory_space=pltpu.VMEM)
    smem = pl.BlockSpec(memory_space=pltpu.SMEM)
    hbm = pl.BlockSpec(memory_space=pl.ANY)
    coulomb, coeffs = pl.pallas_call(
        kernel,
        out_shape=(
            jax.ShapeDtypeStruct((OWN, ND, BS), BF16),
            jax.ShapeDtypeStruct((ND, AUX), F32),
        ),
        in_specs=[smem, smem, hbm, hbm, hbm],
        out_specs=(vmem, vmem),
        scratch_shapes=[
            pltpu.VMEM((ROWS, AUX), BF16),
            pltpu.VMEM((2048, 16, BS), BF16),
            pltpu.VMEM((ND, ROWS), BF16),
            pltpu.VMEM((2, ND, 256), F32),
            pltpu.VMEM((2, 2, ND, 256), F32),
            pltpu.VMEM((8, 8, HALF), F32),
            pltpu.VMEM((7, 8, HALF), F32),
            pltpu.VMEM((1280, 3 * HB), F32),
            pltpu.VMEM((5, 512, 256), BF16),
            pltpu.VMEM((5, 512, 256), BF16),
            pltpu.VMEM((8, 3 * HALF), F32),
            pltpu.VMEM((8, 3 * HALF), F32),
            pltpu.VMEM((16, 3 * HALF), F32),
            pltpu.VMEM((8, HALF), F32),
            pltpu.VMEM((2, 8, HALF), F32),
            pltpu.VMEM((2, 8, 8, HALF), F32),
            pltpu.VMEM((2, 8, 16, 256), BF16),
            pltpu.VMEM((ND, AUX), BF16),
            pltpu.VMEM((2, ZS, ND, BS), F32),
            pltpu.VMEM((2, XS, ND, BS), F32),
            pltpu.VMEM((2, ZS, ND, BS), BF16),
            pltpu.VMEM((2, ZS, ND, BS), BF16),
            pltpu.VMEM((4, ZS, ND, BS), BF16),
            pltpu.VMEM((4, ZS, ND, BS), BF16),
            pltpu.VMEM((ZS, ND, BS), BF16),
            pltpu.VMEM((ZS, ND, BS), BF16),
            pltpu.VMEM((2, ZS, ND, BS), F32),
            pltpu.VMEM((4, XS, ND, BS), BF16),
            pltpu.VMEM((4, XS, ND, BS), BF16),
            pltpu.VMEM((XS, ND, BS), BF16),
            pltpu.VMEM((XS, ND, BS), BF16),
            pltpu.VMEM((2, XS, ND, BS), BF16),
            pltpu.VMEM((2, XS, ND, BS), BF16),
            pltpu.VMEM((XS, ND, BS), F32),
            pltpu.SMEM((4 * SLOTS,), jnp.int32),
            pltpu.SemaphoreType.DMA((NCHUNK,)),
            pltpu.SemaphoreType.DMA((4,)),
            pltpu.SemaphoreType.DMA((NSEMS,)),
            pltpu.SemaphoreType.DMA((NSEMS,)),
        ],
        compiler_params=pltpu.CompilerParams(
            collective_id=0, has_side_effects=True, vmem_limit_bytes=56 * 1024 * 1024
        ),
        cost_estimate=pl.CostEstimate(flops=4 * ND * ROWS * AUX, bytes_accessed=2 * ROWS * AUX, transcendentals=0),
    )(block_list, block_sizes, density.reshape(16, 16, BS), slab, metric)
    return pl.pallas_call(
        deliver,
        out_shape=(
            jax.ShapeDtypeStruct(coulomb.shape, coulomb.dtype),
            jax.ShapeDtypeStruct(coeffs.shape, coeffs.dtype),
        ),
        in_specs=[vmem, vmem],
        out_specs=(vmem, vmem),
    )(coulomb, coeffs)


def solution(mesh):
    return jax.shard_map(
        shards,
        mesh=mesh,
        in_specs=(
            P("pair", "aux"),
            P(("pair", "aux"), None, None),
            P("pair"),
            P("pair"),
            P("aux", None),
        ),
        out_specs=(P(("pair", "aux"), None, None), P(None, "aux")),
        check_vma=False,
    )
```
